256 devices in a mesh: dom: 256 (over z, x, y, core).
Axes of the slice: x: 4, y: 4, z: 8, core: 2. Of those that a mesh axis runs over, the one named last changes fastest.
Arguments:
- embeddings: float32 [65536, 400], P('dom')
- entity_state: float32 [65536], P('dom'), may hold values from 0.0001 to 0.01
- relations: float32 [1300, 400], replicated, may hold values from 0.1 to 1.9
- relation_state: float32 [1300], replicated, may hold values from 0.01 to 1
- round_masks: int32 [2], replicated, may hold values from 1 to 255
- edge_src: int32 [2, 32768], P(None, 'dom'), may hold values from 0 to 255
- edge_rel: int32 [2, 32768], P(None, 'dom'), may hold values from 0 to 1299
- edge_dst: int32 [2, 32768], P(None, 'dom'), may hold values from 0 to 255
- edge_count: int32 [2, 256], P(None, 'dom'), may hold values from 64 to 128, as said below
- neg_rows: int32 [2, 256, 1000], P(None, 'dom'), may hold values from 0 to 255
Outputs:
- new_embeddings: float32 [65536, 400], P('dom')
- new_entity_state: float32 [65536], P('dom')
- new_relations: float32 [1300, 400], replicated
- new_relation_state: float32 [1300], replicated
The draws below stay inside these ranges and needn't reach their ends.
Inputs may be any that keep to these rules, and one draw needn't show every extreme that they name: In round r, device p (partition p) trains the bucket of its own partition with partition p XOR round_masks[r]. A bucket's live edges are its first edge_count slots; in every round some device has exactly 128. `edge_src`: rows of the device's own partition; slots past the count are padding. `edge_dst`: rows of the partner partition of that round. `neg_rows`: row p + c lists the negatives of block c of device p, as rows of the partner partition.
All inputs are finite; a program needn't handle non-finite values.
Results may differ from the reference program's by a relative error of at most 0.0033.
The reference program's roundings to bfloat16 on the way count: a program that leaves them out, or rounds other values in their place, can miss the bound.
Values may be sent and summed in bfloat16 or wider, within the bound.
A program may use at most 64 MiB of HBM per device.

```python
import math
import jax
import jax.numpy as jnp
import numpy as np
from jax import lax

D = 400
NREL = 1300
NEG = 1000
ROUNDS = 2
ROWS_DEV = 256
EDGE_CAP = 128
NCHUNK = 1
ENTITIES = 65536
EDGES = 32768
NEG_LISTS = 256
N_DOM = 256


def draw_embeddings(key, part):
    key = jax.random.fold_in(key, 3)
    key_base = jax.random.fold_in(key, 0)
    key_rows = jax.random.fold_in(key, 2)
    row_scale = jnp.exp(jax.random.uniform(key_rows, (ENTITIES, 1), jnp.float32, -1.15, 1.15))
    base = jax.random.normal(key_base, (ENTITIES, D), jnp.float32)
    return (0.3 * base * row_scale).astype(jnp.float32)


def draw_edge_count(key, part):
    key = jax.random.fold_in(key, 7)
    key_base, key_busy = jax.random.split(key)
    counts = jax.random.randint(key_base, (ROUNDS, N_DOM), EDGE_CAP // 2, EDGE_CAP + 1)
    busiest = jax.random.randint(key_busy, (ROUNDS, 4), 0, N_DOM)
    round_rows = jnp.arange(ROUNDS)[:, None]
    return counts.at[round_rows, busiest].set(EDGE_CAP).astype(jnp.int32)


def plant(values, stream_key, least, high):
    longest = values.shape.index(max(values.shape))
    spots = []
    for shift in (0, 1):
        where = [jax.random.randint(jax.random.fold_in(stream_key, axis), (), 0, length) for axis, length in enumerate(values.shape)]
        where[longest] = (where[longest] + shift) % values.shape[longest]
        spots.append(tuple(where))
    return values.at[spots[0]].set(least).at[spots[1]].set(high)


def block_scale(rng, extent, cuts, smallest, largest):
    level, own = 1.0, jax.random.fold_in(rng, 6)
    for axis_at, parts in cuts:
        steps = jnp.exp(jax.random.uniform(jax.random.fold_in(own, axis_at), (parts,), jnp.float32, smallest / len(cuts), largest / len(cuts)))
        level = level * jnp.repeat(steps, extent[axis_at] // parts).reshape([-1 if axis == axis_at else 1 for axis in range(len(extent))])
    return level


def cumulative_ranks(amount, lean):
    portions = [(1 << 20) // math.isqrt(grade ** lean) + 1 for grade in range(1, amount + 1)]
    spread = 1 + sum(portions) // (1 << 30)
    return np.cumsum(np.array([max(1, weight // spread) for weight in portions]))


def ranked_ids(rng, dims, count, lean):
    table = cumulative_ranks(count, lean)
    lot = jax.random.randint(jax.random.fold_in(rng, 1), dims, 0, int(table[count - 1]))
    grade = jnp.searchsorted(jnp.asarray(table, jnp.int32), lot, side="right")
    return jax.random.permutation(jax.random.fold_in(rng, 2), count)[grade].astype(jnp.int32)


def setup_inputs(seed: int = 0) -> dict:
    keys = jax.random.split(jax.random.key(seed), 11)
    return {
        "embeddings": draw_embeddings(jax.random.fold_in(keys[10], 71), 0),
        "entity_state": jnp.clip(jnp.exp(math.log(0.01) - 4.6051702 * jax.random.uniform(keys[1], (ENTITIES,), jnp.float32) ** block_scale(keys[1], (ENTITIES,), ((0, 256),), -0.2, 0.2)), 0.0001, 0.01),
        "relations": jnp.clip(1.0 + 0.18 * jax.random.normal(keys[2], (NREL, D), jnp.float32), 0.1, 1.9),
        "relation_state": jnp.clip(jnp.exp(jax.random.uniform(keys[3], (NREL,), jnp.float32, math.log(0.01), math.log(1.0))), 0.01, 1.0),
        "round_masks": jax.random.randint(keys[4], (ROUNDS,), 1, N_DOM).astype(jnp.int32),
        "edge_src": plant(jax.random.randint(keys[5], (ROUNDS, EDGES), 0, ROWS_DEV), jax.random.fold_in(keys[5], 1), 0, ROWS_DEV - 1).astype(jnp.int32),
        "edge_rel": plant(ranked_ids(keys[6], (ROUNDS, EDGES), NREL, 2), jax.random.fold_in(keys[6], 3), 0, NREL - 1).astype(jnp.int32),
        "edge_dst": plant(jax.random.randint(keys[7], (ROUNDS, EDGES), 0, ROWS_DEV), jax.random.fold_in(keys[7], 1), 0, ROWS_DEV - 1).astype(jnp.int32),
        "edge_count": draw_edge_count(jax.random.fold_in(keys[10], 71), 0),
        "neg_rows": plant(jax.random.randint(keys[9], (ROUNDS, NEG_LISTS, NEG), 0, ROWS_DEV), jax.random.fold_in(keys[9], 1), 0, ROWS_DEV - 1).astype(jnp.int32),
    }


learning_rate = 0.1

def bucket_grads(vectors, dst_ids, live_edges, neg_ids, table):
    groups, negatives = neg_ids.shape
    edge_total, features = vectors.shape
    per_group = edge_total // groups
    target = table[dst_ids]
    positive = lax.optimization_barrier(jnp.sum(vectors.astype(jnp.float32) * target.astype(jnp.float32), axis=1))
    pos_coef = -live_edges * jax.nn.sigmoid(-positive)
    blocks = vectors.reshape(groups, per_group, features).astype(jnp.float32)
    neg_table = table[neg_ids].astype(jnp.float32)
    scores = jnp.einsum('ced,cnd->cen', blocks, neg_table)
    neg_coef = (live_edges.reshape(groups, per_group, 1) * jax.nn.sigmoid(scores) / negatives).astype(jnp.bfloat16)
    coef_wide = neg_coef.astype(jnp.float32)
    neg_pull = jnp.einsum('cen,cnd->ced', coef_wide, neg_table).reshape(edge_total, features)
    vec_grads = (pos_coef[:, None] * target.astype(jnp.float32) + neg_pull).astype(jnp.bfloat16)
    row_terms = jnp.einsum('cen,ced->cnd', coef_wide, blocks).reshape(groups * negatives, features)
    dest_grads = jnp.zeros((table.shape[0], features), jnp.float32)
    dest_grads = dest_grads.at[dst_ids].add(pos_coef[:, None] * vectors.astype(jnp.float32))
    dest_grads = dest_grads.at[neg_ids.reshape(-1)].add(row_terms)
    return (vec_grads, dest_grads.astype(jnp.bfloat16))

def reference(embeddings, entity_state, relations, relation_state, round_masks, edge_src, edge_rel, edge_dst, edge_count, neg_rows):
    entity_rows = embeddings
    row_state = entity_state.reshape(N_DOM, ROWS_DEV)
    rel_sum = jnp.zeros((NREL, D), jnp.float32)
    devices = jnp.arange(N_DOM, dtype=jnp.int32)
    slot_index = jnp.arange(EDGE_CAP, dtype=jnp.int32)
    for round_index in range(ROUNDS):
        own_rows = entity_rows.reshape(N_DOM, ROWS_DEV, D)
        rows_bf = own_rows.astype(jnp.bfloat16)
        partners = jnp.bitwise_xor(devices, round_masks[round_index]).astype(jnp.int32)
        src_all = edge_src[round_index].reshape(N_DOM, EDGE_CAP)
        rel_all = edge_rel[round_index].reshape(N_DOM, EDGE_CAP)
        dst_all = edge_dst[round_index].reshape(N_DOM, EDGE_CAP)
        neg_all = neg_rows[round_index].reshape(N_DOM, NCHUNK, NEG)
        counts = edge_count[round_index]

        def device_step(carry, items):
            device, partner, src_ids, rel_ids, dst_ids, live_count, neg_ids = items
            own_part = own_rows[device]
            src_rows = own_part[src_ids]
            rel_rows = relations[rel_ids]
            vectors = (src_rows * rel_rows).astype(jnp.bfloat16)
            live_edges = (slot_index < live_count).astype(jnp.float32)
            vec_grads, dest_grads = bucket_grads(vectors, dst_ids, live_edges, neg_ids, rows_bf[partner])
            grad_wide = vec_grads.astype(jnp.float32)
            src_grads = jnp.zeros((ROWS_DEV, D), jnp.float32).at[src_ids].add(grad_wide * rel_rows)
            carry = carry.at[rel_ids].add(grad_wide * src_rows)
            return (carry, (src_grads, dest_grads))
        rel_sum, outputs = lax.scan(device_step, rel_sum, (devices, partners, src_all, rel_all, dst_all, counts, neg_all))
        src_grads, dest_grads = outputs
        row_grads = src_grads + dest_grads[partners].astype(jnp.float32)
        row_state = row_state + lax.optimization_barrier(jnp.mean(row_grads * row_grads, axis=2))
        own_rows = own_rows - learning_rate * row_grads / jnp.sqrt(row_state)[:, :, None]
        entity_rows = own_rows.reshape(ENTITIES, D)
    new_state = relation_state + lax.optimization_barrier(jnp.mean(rel_sum * rel_sum, axis=1))
    new_relations = relations - learning_rate * rel_sum / jnp.sqrt(new_state)[:, None]
    return (entity_rows, row_state.reshape(ENTITIES), new_relations, new_state)
```

```python
import jax
import jax.numpy as jnp
from jax import lax
from jax.experimental import pallas as pl
from jax.experimental.pallas import tpu as pltpu
from jax.sharding import PartitionSpec as P

ROUNDS = 2
D = 400
NREL = 1300
NEG = 1000
ROWS = 256
EDGES = 128
WIDE = 512
LEFT = D - 384
TILES = 32
BLOCK = 1304
GROUP = 168
PACKED = 4096

learning_rate = 0.1

F32 = jnp.float32
BF16 = jnp.bfloat16


def iota(shape, dim):
    return lax.broadcasted_iota(jnp.int32, shape, dim)


def dot(a, b, left=1, right=0):
    return lax.dot_general(a, b, (((left,), (right,)), ((), ())), preferred_element_type=F32)


def halves(value):
    high = value.astype(BF16)
    return high, (value - high.astype(F32)).astype(BF16)


def as_column(row):
    count = row.shape[1]
    square = (count, count)
    return jnp.sum(jnp.where(iota(square, 0) == iota(square, 1), row, 0.0), axis=1, keepdims=True)


def as_row(column):
    count = column.shape[0]
    square = (count, count)
    return jnp.sum(jnp.where(iota(square, 0) == iota(square, 1), column, 0.0), axis=0, keepdims=True)


def remote(source, target, send, recv, device):
    return pltpu.make_async_remote_copy(
        src_ref=source,
        dst_ref=target,
        send_sem=send,
        recv_sem=recv,
        device_id=(device,),
        device_id_type=pl.DeviceIdType.MESH,
    )


def await_bytes(ref, sem):
    pltpu.make_async_copy(ref, ref, sem).wait()


def kernel(
    masks,
    src_ids,
    rel_ids,
    counts,
    emb_in,
    state_in,
    relations,
    rel_state_in,
    src_rows,
    rel_rows,
    dst_rows,
    neg_rows,
    emb_out,
    state_out,
    rel_out,
    rel_state_out,
    emb,
    srcs,
    rels,
    block,
    dest,
    grads,
    packed,
    state_col,
    x1,
    b1,
    x2,
    b2,
    x3,
    b3,
    t0,
    r0,
    t1,
    ra,
    t2,
    rb,
    t3,
    rz,
    gathered,
    send,
    recv,
    sum_send,
    sum_recv,
):
    me = lax.axis_index("dom")
    a = me // 8
    b = me % 8
    c = me % 2
    y = (me // 2) % 4
    x = (me // 8) % 4
    z = me // 32

    barrier = pltpu.get_barrier_semaphore()

    def tell(device):
        pl.semaphore_signal(barrier, inc=1, device_id=(device,), device_id_type=pl.DeviceIdType.MESH)

    def tell_a(step, _):
        tell(((a + step) % 32) * 8 + b)
        return 0

    def tell_b(step, _):
        tell(a * 8 + (b + step) % 8)
        return 0

    def tell_c(step, _):
        device = ((a + step) % 32) * 8 + a % 8

        @pl.when(device != me)
        def _():
            tell(device)

        return 0

    lax.fori_loop(1, 32, tell_a, 0)
    lax.fori_loop(1, 8, tell_b, 0)
    lax.fori_loop(0, 32, tell_c, 0)

    def gather_rels(r):
        rels[r, :, 384:] = jnp.zeros((EDGES, 128), F32)
        for e in range(EDGES):
            rels[r, e : e + 1, :D] = relations[pl.ds(rel_ids[r, e], 1), :]

    def gather_srcs(r):
        for e in range(EDGES):
            srcs[r, e : e + 1, :] = emb[pl.ds(src_ids[r, e], 1), :]

    def vectors_out(r):
        values = srcs[r] * rels[r]
        dst = as_column(dst_rows[r : r + 1, :].astype(F32))
        live = (iota((EDGES, 1), 0) < counts[r, 0]).astype(F32)
        negatives = neg_rows[r : r + 1, :]
        hits = jnp.sum((iota((ROWS, NEG), 0) == negatives).astype(F32), axis=1, keepdims=True)
        high = jnp.floor(hits * (1.0 / 16.0))
        low = hits - 16.0 * high
        lane = iota((EDGES, 128), 1)
        last = values[:, 384:]
        extras = (dst, live, high[:128], high[128:], low[:128], low[128:])
        for n, extra in enumerate(extras):
            last = jnp.where(lane == LEFT + n, extra, last)
        put_block(2 * r, values[:, :384].astype(BF16), last.astype(BF16))

    def put_block(k, main, last):
        for i in range(8):
            for j in range(4):
                part = main[16 * i : 16 * i + 16, 128 * j : 128 * j + 128] if j < 3 else last[16 * i : 16 * i + 16]
                x1[k, 4 * i + j] = part

    def exchange(k, mask, during=None):
        mask_a = lax.shift_right_logical(mask, 3)
        mask_b = lax.bitwise_and(mask, 7)

        def first(step, _):
            t = (a + step) % 32
            remote(x1.at[k, t], b1.at[k, a], send.at[k, 0], recv.at[k, 0], t * 8 + b).start()
            return 0

        lax.fori_loop(1, 32, first, 0)
        b1[k, a] = x1[k, a]
        if during is not None:
            during()
        await_bytes(b1.at[k, pl.ds(0, 31)], recv.at[k, 0])

        for low in range(8):
            for h in range(4):
                x2[k, 4 * low + h] = b1[k, lax.bitwise_xor(mask_a, 8 * h + low)]

        def second(step, _):
            to = (b + step) % 8
            remote(
                x2.at[k, pl.ds(4 * to, 4)],
                b2.at[k, pl.ds(4 * b, 4)],
                send.at[k, 1],
                recv.at[k, 1],
                a * 8 + to,
            ).start()
            return 0

        lax.fori_loop(1, 8, second, 0)
        b2[k, pl.ds(4 * b, 4)] = x2[k, pl.ds(4 * b, 4)]
        await_bytes(b2.at[k, pl.ds(0, 28)], recv.at[k, 1])

        for to in range(8):
            from_b = lax.bitwise_xor(mask_b, to)
            x3[k, 4 * to : 4 * to + 4] = b2[k, pl.ds(4 * from_b, 4)]

        def third(step, _):
            n = (a + step) % 32
            h = n // 8
            to = n % 8
            device = (8 * h + b) * 8 + to

            @pl.when(device != me)
            def _():
                remote(x3.at[k, 4 * to + h], b3.at[k, a], send.at[k, 2], recv.at[k, 2], device).start()

            @pl.when(device == me)
            def _():
                b3[k, a] = x3[k, 4 * to + h]

            return 0

        lax.fori_loop(0, 32, third, 0)

        @pl.when(a % 8 == b)
        def _():
            await_bytes(b3.at[k, pl.ds(0, 31)], recv.at[k, 2])

        @pl.when(a % 8 != b)
        def _():
            await_bytes(b3.at[k], recv.at[k, 2])

        for i in range(8):
            for j in range(4):
                block[16 * i : 16 * i + 16, 128 * j : 128 * j + 128] = b3[k, 4 * i + j]

    def sent(k):
        await_bytes(x1.at[k, pl.ds(0, 31)], send.at[k, 0])
        await_bytes(x2.at[k, pl.ds(0, 28)], send.at[k, 1])

        @pl.when(a % 8 == b)
        def _():
            await_bytes(x3.at[k, pl.ds(0, 31)], send.at[k, 2])

        @pl.when(a % 8 != b)
        def _():
            await_bytes(x3.at[k], send.at[k, 2])

    emb[:, 384:] = jnp.zeros((ROWS, 128), F32)
    emb[:, :D] = emb_in[...]
    gather_rels(0)
    gather_srcs(0)
    vectors_out(0)
    state = jnp.concatenate([as_column(state_in[:, :128]), as_column(state_in[:, 128:])], axis=0)
    for n in range(11):
        width = min(128, NREL - 128 * n)
        part = rel_state_in[:, 128 * n : 128 * n + width]
        if width < 128:
            part = jnp.concatenate([part, jnp.ones((1, 128 - width), F32)], axis=1)
        state_col[128 * n : 128 * n + 128, :] = as_column(part)

    @pl.when(a % 8 == b)
    def _():
        pl.semaphore_wait(barrier, 31 + 7 + 31)

    @pl.when(a % 8 != b)
    def _():
        pl.semaphore_wait(barrier, 31 + 7 + 32)

    for r in range(ROUNDS):
        mask = masks[r]
        exchange(2 * r, mask, (lambda: gather_rels(1)) if r == 0 else None)

        vec = block[...]
        table = emb[...].astype(BF16)
        scores = dot(vec, table, 1, 1)
        meta = vec[:, 384:].astype(F32)
        dst = meta[:, LEFT : LEFT + 1]
        live = meta[:, LEFT + 1 : LEFT + 2]
        hits = [
            as_row(16.0 * meta[:, LEFT + 2 + n : LEFT + 3 + n] + meta[:, LEFT + 4 + n : LEFT + 5 + n])
            for n in range(2)
        ]
        hits = jnp.concatenate(hits, axis=1)
        is_dst = iota((EDGES, ROWS), 1).astype(F32) == dst
        neg_coef = (live * (1.0 / (1.0 + jnp.exp(-scores))) / NEG).astype(BF16).astype(F32)
        positive = jnp.sum(jnp.where(is_dst, scores, 0.0), axis=1, keepdims=True)
        pos_coef = -live * (1.0 / (1.0 + jnp.exp(positive)))
        coef = neg_coef * hits + jnp.where(is_dst, pos_coef, 0.0)
        coef_high, coef_low = halves(coef)
        pulled = (dot(coef_high, table) + dot(coef_low, table)).astype(BF16)
        put_block(2 * r + 1, pulled[:, :384], pulled[:, 384:])

        def dest_part(vec=vec, coef_high=coef_high, coef_low=coef_low):
            total = dot(coef_high, vec, 0, 0) + dot(coef_low, vec, 0, 0)
            total = total.astype(BF16).astype(F32)
            dest[...] = jnp.where(iota((ROWS, WIDE), 1) < D, total, 0.0)

        exchange(2 * r + 1, mask, dest_part)

        wide = block[...].astype(F32)
        grads[r * EDGES : (r + 1) * EDGES, :] = wide * srcs[r]
        is_src = (iota((ROWS, EDGES), 0) == src_rows[r : r + 1, :]).astype(BF16)
        high, low = halves(wide * rels[r])
        grad = dest[...] + dot(is_src, high) + dot(is_src, low)
        state = state + jnp.sum(grad * grad, axis=1, keepdims=True) * (1.0 / D)
        emb[...] = emb[...] - learning_rate * grad / jnp.sqrt(state)
        if r + 1 < ROUNDS:
            gather_srcs(r + 1)
            vectors_out(r + 1)

    high, low = halves(grads[...])
    ids = jnp.concatenate([rel_rows[0:1, :], rel_rows[1:2, :]], axis=1)
    tail = jnp.zeros((GROUP, 128), F32)
    for g in range(8):
        rows = min(GROUP, BLOCK - GROUP * g)
        is_rel = (iota((GROUP, ROUNDS * EDGES), 0) + GROUP * g == ids).astype(BF16)
        part = dot(is_rel, high) + dot(is_rel, low)
        for n in range(3):
            at = BLOCK * n + GROUP * g
            packed[at : at + rows, :] = part[:rows, 128 * n : 128 * n + 128]
        end = part[:, 384:]
        tail = tail + (pltpu.roll(end, LEFT * g, 1) if g else end)
    packed[3 * BLOCK : 3 * BLOCK + GROUP, :] = tail
    packed[3 * BLOCK + GROUP :, :] = jnp.zeros((PACKED - 3 * BLOCK - GROUP, 128), F32)
    t0[...] = packed[...].reshape(256, 16, 128).astype(BF16)

    def at_x(to):
        return ((z * 4 + to) * 4 + y) * 2 + c

    def at_y(to):
        return ((z * 4 + x) * 4 + to) * 2 + c

    def at_z(to):
        return ((to * 4 + x) * 4 + y) * 2 + c

    other = me + 1 - 2 * c

    remote(t0.at[pl.ds((1 - c) * 128, 128)], r0, sum_send.at[0], sum_recv.at[0], other).start()
    await_bytes(r0, sum_recv.at[0])
    t1[...] = (t0[pl.ds(c * 128, 128)].astype(F32) + r0[...].astype(F32)).astype(BF16)

    for step in range(1, 4):
        to_x, to_y = (x + step) % 4, (y + step) % 4
        remote(t1.at[pl.ds(16 * to_x, 16)], ra.at[0, x], sum_send.at[1], sum_recv.at[1], at_x(to_x)).start()
        remote(t1.at[pl.ds(64 + 16 * to_y, 16)], ra.at[1, y], sum_send.at[2], sum_recv.at[2], at_y(to_y)).start()
    ra[0, x] = t1[pl.ds(16 * x, 16)]
    ra[1, y] = t1[pl.ds(64 + 16 * y, 16)]

    def added(ref, lead, count):
        total = ref[lead + (0,)].astype(F32)
        for n in range(1, count):
            total = total + ref[lead + (n,)].astype(F32)
        return total.astype(BF16)

    await_bytes(ra.at[0, pl.ds(0, 3)], sum_recv.at[1])
    t2[0] = added(ra, (0,), 4)
    for step in range(1, 4):
        to_y = (y + step) % 4
        remote(t2.at[0, pl.ds(4 * to_y, 4)], rb.at[0, y], sum_send.at[3], sum_recv.at[3], at_y(to_y)).start()
    rb[0, y] = t2[0, pl.ds(4 * y, 4)]
    await_bytes(ra.at[1, pl.ds(0, 3)], sum_recv.at[2])
    t2[1] = added(ra, (1,), 4)
    for step in range(1, 4):
        to_x = (x + step) % 4
        remote(t2.at[1, pl.ds(4 * to_x, 4)], rb.at[1, x], sum_send.at[4], sum_recv.at[4], at_x(to_x)).start()
    rb[1, x] = t2[1, pl.ds(4 * x, 4)]
    await_bytes(rb.at[0, pl.ds(0, 3)], sum_recv.at[3])
    t3[0:4] = added(rb, (0,), 4)
    await_bytes(rb.at[1, pl.ds(0, 3)], sum_recv.at[4])
    t3[4:8] = added(rb, (1,), 4)

    def spread_z(step, _):
        to = (z + step) % 8
        remote(t3.at[to], rz.at[z], sum_send.at[5], sum_recv.at[5], at_z(to)).start()
        return 0

    lax.fori_loop(1, 8, spread_z, 0)
    rz[z] = t3[z]
    await_bytes(rz.at[pl.ds(0, 7)], sum_recv.at[5])

    which = z // 4
    base_x = c * 128 + 16 * x + 4 * y
    base_y = c * 128 + 64 + 16 * y + 4 * x
    mine = (1 - which) * base_x + which * base_y + z % 4
    gathered[mine] = added(rz, (), 8)

    def gather_z(step, _):
        to = (z + step) % 8
        remote(gathered.at[mine], gathered.at[mine], sum_send.at[6], sum_recv.at[6], at_z(to)).start()
        return 0

    lax.fori_loop(1, 8, gather_z, 0)
    await_bytes(gathered.at[pl.ds(0, 7)], sum_recv.at[6])

    def whole(first, count, n, device):
        part = gathered.at[pl.ds(first, count)]
        return remote(part, part, sum_send.at[n], sum_recv.at[n], device)

    for step in range(1, 4):
        to_x, to_y = (x + step) % 4, (y + step) % 4
        whole(base_x, 4, 7, at_y(to_y)).start()
        whole(base_y, 4, 8, at_x(to_x)).start()
    await_bytes(gathered.at[pl.ds(0, 12)], sum_recv.at[7])
    await_bytes(gathered.at[pl.ds(0, 12)], sum_recv.at[8])
    for step in range(1, 4):
        to_x, to_y = (x + step) % 4, (y + step) % 4
        whole(c * 128 + 16 * x, 16, 9, at_x(to_x)).start()
        whole(c * 128 + 64 + 16 * y, 16, 10, at_y(to_y)).start()
    await_bytes(gathered.at[pl.ds(0, 48)], sum_recv.at[9])
    await_bytes(gathered.at[pl.ds(0, 48)], sum_recv.at[10])
    whole(c * 128, 128, 11, other).start()
    emb_out[...] = emb[:, :D]
    state_out[...] = jnp.concatenate([as_row(state[:128]), as_row(state[128:])], axis=1)
    await_bytes(gathered.at[pl.ds(0, 128)], sum_recv.at[11])

    packed[...] = gathered[...].astype(F32).reshape(PACKED, 128)
    for g in range(8):
        rows = min(GROUP, NREL - GROUP * g)
        at = GROUP * g
        parts = [packed[BLOCK * n + at : BLOCK * n + at + rows, :] for n in range(3)]
        end = packed[3 * BLOCK : 3 * BLOCK + GROUP, :]
        end = (pltpu.roll(end, 128 - LEFT * g, 1) if g else end)[:rows, :LEFT]
        squares = parts[0] * parts[0] + parts[1] * parts[1] + parts[2] * parts[2]
        mean = jnp.sum(squares, axis=1, keepdims=True) + jnp.sum(end * end, axis=1, keepdims=True)
        fresh = state_col[at : at + rows, :] + mean * (1.0 / D)
        state_col[at : at + rows, :] = fresh
        root = jnp.sqrt(fresh)
        for n in range(3):
            cols = slice(128 * n, 128 * n + 128)
            rel_out[at : at + rows, cols] = relations[at : at + rows, cols] - learning_rate * parts[n] / root
        rel_out[at : at + rows, 384:] = relations[at : at + rows, 384:] - learning_rate * end / root
    for n in range(11):
        width = min(128, NREL - 128 * n)
        row = as_row(state_col[128 * n : 128 * n + 128, :])
        rel_state_out[:, 128 * n : 128 * n + width] = row[:, :width]

    for k in range(2 * ROUNDS):
        sent(k)
    await_bytes(t0.at[pl.ds(0, 128)], sum_send.at[0])
    for n, tiles in ((1, 48), (2, 48), (3, 12), (4, 12), (5, 7), (6, 7), (7, 12), (8, 12), (9, 48), (10, 48), (11, 128)):
        await_bytes(gathered.at[pl.ds(0, tiles)], sum_send.at[n])


def shards(
    embeddings,
    entity_state,
    relations,
    relation_state,
    round_masks,
    edge_src,
    edge_rel,
    edge_dst,
    edge_count,
    neg_rows,
):
    smem = pl.BlockSpec(memory_space=pltpu.SMEM)
    vmem = pl.BlockSpec(memory_space=pltpu.VMEM)

    def tiles(*lead):
        return pltpu.VMEM(lead + (16, 128), BF16)

    new_rows, new_state, new_relations, new_relation_state = pl.pallas_call(
        kernel,
        out_shape=(
            jax.ShapeDtypeStruct((ROWS, D), F32),
            jax.ShapeDtypeStruct((1, ROWS), F32),
            jax.ShapeDtypeStruct((NREL, D), F32),
            jax.ShapeDtypeStruct((1, NREL), F32),
        ),
        in_specs=[smem] * 4 + [vmem] * 8,
        out_specs=(vmem,) * 4,
        scratch_shapes=[
            pltpu.VMEM((ROWS, WIDE), F32),
            pltpu.VMEM((ROUNDS, EDGES, WIDE), F32),
            pltpu.VMEM((ROUNDS, EDGES, WIDE), F32),
            pltpu.VMEM((EDGES, WIDE), BF16),
            pltpu.VMEM((ROWS, WIDE), F32),
            pltpu.VMEM((ROUNDS * EDGES, WIDE), F32),
            pltpu.VMEM((PACKED, 128), F32),
            pltpu.VMEM((1408, 1), F32),
        ]
        + [tiles(2 * ROUNDS, TILES)] * 6
        + [
            tiles(256),
            tiles(128),
            tiles(128),
            tiles(2, 4, 16),
            tiles(2, 16),
            tiles(2, 4, 4),
            tiles(8),
            tiles(8),
            tiles(256),
            pltpu.SemaphoreType.DMA((2 * ROUNDS, 3)),
            pltpu.SemaphoreType.DMA((2 * ROUNDS, 3)),
            pltpu.SemaphoreType.DMA((12,)),
            pltpu.SemaphoreType.DMA((12,)),
        ],
        compiler_params=pltpu.CompilerParams(
            collective_id=0, has_side_effects=True, vmem_limit_bytes=48 * 1024 * 1024
        ),
    )(
        round_masks,
        edge_src,
        edge_rel,
        edge_count,
        embeddings,
        entity_state.reshape(1, ROWS),
        relations,
        relation_state.reshape(1, NREL),
        edge_src,
        edge_rel,
        edge_dst,
        neg_rows.reshape(ROUNDS, NEG),
    )
    return (new_rows, new_state.reshape(ROWS), new_relations, new_relation_state.reshape(NREL))


def solution(mesh):
    placed = (
        P("dom", None),
        P("dom"),
        P(),
        P(),
        P(),
        P(None, "dom"),
        P(None, "dom"),
        P(None, "dom"),
        P(None, "dom"),
        P(None, "dom", None),
    )
    return jax.shard_map(
        shards,
        mesh=mesh,
        in_specs=placed,
        out_specs=(P("dom", None), P("dom"), P(), P()),
        check_vma=False,
    )
```

```python
import jax
import jax.numpy as jnp
from jax import lax
from jax.experimental import pallas as pl
from jax.experimental.pallas import tpu as pltpu
from jax.sharding import PartitionSpec as P

ROUNDS = 2
D = 400
NREL = 1300
NEG = 1000
ROWS = 256
EDGES = 128
WIDE = 512
LEFT = D - 384
DEVICES = 256
TILES = 76
REL_PAD = 1408
BLOCK = 1304
GROUP = 168
PACKED = 4096

learning_rate = 0.1

F32 = jnp.float32
BF16 = jnp.bfloat16


def iota(shape, dim):
    return lax.broadcasted_iota(jnp.int32, shape, dim)


def dot(a, b, left=1, right=0):
    return lax.dot_general(a, b, (((left,), (right,)), ((), ())), preferred_element_type=F32)


def halves(value):
    high = value.astype(BF16)
    return high, (value - high.astype(F32)).astype(BF16)


def as_column(row):
    count = row.shape[1]
    square = (count, count)
    return jnp.sum(jnp.where(iota(square, 0) == iota(square, 1), row, 0.0), axis=1, keepdims=True)


def as_row(column):
    count = column.shape[0]
    square = (count, count)
    return jnp.sum(jnp.where(iota(square, 0) == iota(square, 1), column, 0.0), axis=0, keepdims=True)


def remote(source, target, send, recv, device):
    return pltpu.make_async_remote_copy(
        src_ref=source,
        dst_ref=target,
        send_sem=send,
        recv_sem=recv,
        device_id=(device,),
        device_id_type=pl.DeviceIdType.MESH,
    )


def await_bytes(ref, sem):
    pltpu.make_async_copy(ref, ref, sem).wait()


def carrier(tile):
    return (10 * tile) // 3


def kernel(
    masks_hbm,
    src_hbm,
    rel_hbm,
    counts_hbm,
    emb_hbm,
    state_hbm,
    relations_hbm,
    rel_state_hbm,
    dst_hbm,
    neg_hbm,
    emb_out,
    state_out,
    rel_out,
    rel_state_out,
    masks,
    src_ids,
    rel_ids,
    counts,
    emb_in,
    state_in,
    rel_in,
    rel_state_in,
    src_rows,
    rel_rows,
    dst_rows,
    neg_rows,
    emb,
    relations,
    srcs,
    rels,
    table,
    vec,
    far_table,
    far_vec,
    grads,
    is_rel,
    packed,
    state_col,
    x1,
    held_0,
    held_1,
    x2,
    arrived,
    t0,
    r0,
    t1,
    ra,
    t2,
    rb,
    t3,
    rz,
    gathered,
    send,
    recv,
    sum_send,
    sum_recv,
    loaded,
):
    loads = [
        pltpu.make_async_copy(source, target, loaded.at[n])
        for n, (source, target) in enumerate(
            (
                (emb_hbm, emb_in),
                (relations_hbm, rel_in),
                (src_hbm, src_ids),
                (rel_hbm, rel_ids),
                (masks_hbm, masks),
                (counts_hbm, counts),
                (state_hbm, state_in),
                (rel_state_hbm, rel_state_in),
                (src_hbm, src_rows),
                (rel_hbm, rel_rows),
                (dst_hbm, dst_rows),
                (neg_hbm, neg_rows),
            )
        )
    ]
    for load in loads:
        load.start()
    me = lax.axis_index("dom")
    c = me % 2
    y = (me // 2) % 4
    x = (me // 8) % 4
    z = me // 32
    mine = (3 * me + 2) // 10
    active = jnp.logical_and(carrier(mine) == me, mine < TILES)
    idle = jnp.logical_not(active)
    first_tile = (me * TILES) // DEVICES

    def at_x(to):
        return ((z * 4 + to) * 4 + y) * 2 + c

    def at_y(to):
        return ((z * 4 + x) * 4 + to) * 2 + c

    def at_z(to):
        return ((to * 4 + x) * 4 + y) * 2 + c

    other = me + 1 - 2 * c

    barrier = pltpu.get_barrier_semaphore()

    def tell(device):
        pl.semaphore_signal(barrier, inc=1, device_id=(device,), device_id_type=pl.DeviceIdType.MESH)

    def tell_all(step, _):
        tell((me + step) % DEVICES)
        return 0

    def tell_carriers(step, _):
        tell(carrier((first_tile + step) % TILES))
        return 0

    @pl.when(active)
    def _():
        lax.fori_loop(1, DEVICES, tell_all, 0)

    @pl.when(idle)
    def _():
        lax.fori_loop(0, TILES, tell_carriers, 0)

    for step in range(1, 4):
        tell(at_x((x + step) % 4))
        tell(at_y((y + step) % 4))
    for step in range(1, 8):
        tell(at_z((z + step) % 8))
    tell(other)

    def gather_rels(r):
        for e in range(EDGES):
            rels[r, e : e + 1, :] = relations[pl.ds(rel_ids[r, e], 1), :]

    def gather_srcs(r):
        for e in range(EDGES):
            srcs[r, e : e + 1, :] = emb[pl.ds(src_ids[r, e], 1), :]

    def hit_row(r):
        hits = jnp.sum((iota((ROWS, NEG), 0) == neg_rows[r]).astype(F32), axis=1, keepdims=True)
        return jnp.concatenate([as_row(hits[:128]), as_row(hits[128:])], axis=1)

    def bucket_rows(r):
        dst = dst_rows[r : r + 1, :].astype(F32)
        live = (iota((1, EDGES), 1) < counts[r]).astype(F32)
        return dst, live, hit_row(r)

    def pack(r, first, rows):
        for i in range(8):
            for j in range(3):
                x1[r, first + 3 * i + j] = rows[16 * i : 16 * i + 16, 128 * j : 128 * j + 128]
        last = rows[:, 384:].astype(F32)
        tail = last[:16]
        for g in range(1, 8):
            tail = tail + pltpu.roll(last[16 * g : 16 * g + 16], LEFT * g, 1)
        x1[r, first + 24] = tail.astype(BF16)

    def unpack(r, first, target, at):
        for i in range(8):
            for j in range(3):
                target[at + 16 * i : at + 16 * i + 16, 128 * j : 128 * j + 128] = arrived[r, first + 3 * i + j]
        tail = arrived[r, first + 24].astype(F32)
        inside = iota((16, 128), 1) < LEFT
        for g in range(8):
            part = pltpu.roll(tail, 128 - LEFT * g, 1) if g else tail
            target[at + 16 * g : at + 16 * g + 16, 384:] = jnp.where(inside, part, 0.0).astype(BF16)

    def pack_table(r):
        table[...] = emb[...].astype(BF16)
        pack(r, 0, table[0:128, :])
        pack(r, 25, table[128:256, :])

    def pack_vectors(r, rows):
        dst, live, hits = rows
        vec[...] = (srcs[r] * rels[r]).astype(BF16)
        pack(r, 50, vec[...])
        high = jnp.floor(hits * (1.0 / 16.0))
        low = hits - 16.0 * high
        extras = (dst, live, high[:, :128], high[:, 128:], low[:, :128], low[:, 128:])
        sub = iota((16, 128), 0)
        meta = jnp.zeros((16, 128), F32)
        for n, extra in enumerate(extras):
            meta = jnp.where(sub == n, extra, meta)
        x1[r, 75] = meta.astype(BF16)

    def exchange(r, mask, during):
        held = (held_0, held_1)[r]

        def outward(step, _):
            i = (first_tile + step) % TILES
            device = carrier(i)

            @pl.when(device != me)
            def _():
                remote(x1.at[r, i], held.at[me], send.at[r, 0], recv.at[r, 0], device).start()

            @pl.when(device == me)
            def _():
                held[me] = x1[r, i]

            return 0

        lax.fori_loop(0, TILES, outward, 0)
        during()

        @pl.when(active)
        def _():
            await_bytes(held.at[pl.ds(0, DEVICES - 1)], recv.at[r, 0])

            def onward(step, _):
                base = 16 * ((me // 16 + step) % 16)
                for n in range(16):
                    x2[r, base + n] = held[lax.bitwise_xor(mask, base + n)]
                for n in range(16):
                    device = base + n

                    @pl.when(device != me)
                    def _():
                        remote(x2.at[r, device], arrived.at[r, mine], send.at[r, 1], recv.at[r, 1], device).start()

                return 0

            lax.fori_loop(0, 16, onward, 0)
            arrived[r, mine] = x2[r, me]
            await_bytes(arrived.at[r, pl.ds(0, TILES - 1)], recv.at[r, 1])

        @pl.when(idle)
        def _():
            await_bytes(arrived.at[r], recv.at[r, 1])

        unpack(r, 0, far_table, 0)
        unpack(r, 25, far_table, 128)
        unpack(r, 50, far_vec, 0)

    def sent(r):
        @pl.when(active)
        def _():
            await_bytes(x1.at[r, pl.ds(0, TILES - 1)], send.at[r, 0])
            await_bytes(x2.at[r, pl.ds(0, DEVICES - 1)], send.at[r, 1])

        @pl.when(idle)
        def _():
            await_bytes(x1.at[r], send.at[r, 0])

    def coefficients(vectors, rows, ends):
        dst, live, hits = ends
        scores = dot(vectors, rows, 1, 1)
        dst = as_column(dst)
        live = as_column(live)
        is_dst = iota((EDGES, ROWS), 1).astype(F32) == dst
        neg_coef = (live * (1.0 / (1.0 + jnp.exp(-scores))) / NEG).astype(BF16).astype(F32)
        positive = jnp.sum(jnp.where(is_dst, scores, 0.0), axis=1, keepdims=True)
        pos_coef = -live * (1.0 / (1.0 + jnp.exp(positive)))
        return halves(neg_coef * hits + jnp.where(is_dst, pos_coef, 0.0))

    for load in loads:
        load.wait()
    emb[:, 384:] = jnp.zeros((ROWS, 128), F32)
    for j in range(4):
        depth = min(128, D - 128 * j)
        for i in range(2):
            emb[128 * i : 128 * i + 128, 128 * j : 128 * j + depth] = emb_in[
                128 * j : 128 * j + depth, 128 * i : 128 * i + 128
            ].T
    pack_table(0)
    relations[:, 384:] = jnp.zeros((REL_PAD, 128), F32)
    for j in range(4):
        depth = min(128, D - 128 * j)
        for i in range(11):
            width = min(128, NREL - 128 * i)
            part = rel_in[128 * j : 128 * j + depth, 128 * i : 128 * i + width]
            if width < 128:
                part = jnp.concatenate([part, jnp.ones((depth, 128 - width), F32)], axis=1)
            relations[128 * i : 128 * i + 128, 128 * j : 128 * j + depth] = part.T
    gather_rels(0)
    gather_srcs(0)
    near = bucket_rows(0)
    pack_vectors(0, near)
    state = jnp.concatenate([as_column(state_in[:, :128]), as_column(state_in[:, 128:])], axis=0)

    @pl.when(active)
    def _():
        pl.semaphore_wait(barrier, DEVICES - 1 + 14)

    @pl.when(idle)
    def _():
        pl.semaphore_wait(barrier, TILES + 14)

    def prepare():
        gather_rels(1)
        later.append(bucket_rows(1))
        for n in range(11):
            width = min(128, NREL - 128 * n)
            part = rel_state_in[128 * n : 128 * n + width].reshape(1, width)
            if width < 128:
                part = jnp.concatenate([part, jnp.ones((1, 128 - width), F32)], axis=1)
            state_col[128 * n : 128 * n + 128, :] = as_column(part)

    def prepare_sum():
        ids = jnp.concatenate([rel_rows[0:1, :], rel_rows[1:2, :]], axis=1)
        for g in range(8):
            at = GROUP * g
            is_rel[at : at + GROUP, :] = (iota((GROUP, ROUNDS * EDGES), 0) + at == ids).astype(BF16)

    later = []
    for r in range(ROUNDS):
        exchange(r, masks[r], prepare if r == 0 else prepare_sum)
        meta = arrived[r, 75].astype(F32)
        hits = jnp.concatenate([16.0 * meta[n : n + 1] + meta[n + 2 : n + 3] for n in (2, 3)], axis=1)
        far = (meta[0:1], meta[1:2], hits)

        high, low = coefficients(vec[...], far_table[...], near)
        pulled = (dot(high, far_table[...]) + dot(low, far_table[...])).astype(BF16).astype(F32)
        high, low = coefficients(far_vec[...], table[...], far)
        pushed = (dot(high, far_vec[...], 0, 0) + dot(low, far_vec[...], 0, 0)).astype(BF16).astype(F32)

        grads[r * EDGES : (r + 1) * EDGES, :] = (pulled * srcs[r]).astype(BF16)
        is_src = (iota((ROWS, EDGES), 0) == src_rows[r : r + 1, :]).astype(BF16)
        high, low = halves(pulled * rels[r])
        grad = pushed + dot(is_src, high) + dot(is_src, low)
        state = state + jnp.sum(grad * grad, axis=1, keepdims=True) * (1.0 / D)
        emb[...] = emb[...] - learning_rate * grad / jnp.sqrt(state)
        if r + 1 < ROUNDS:
            pack_table(r + 1)
            gather_srcs(r + 1)
            near = later[r]
            pack_vectors(r + 1, near)

    tail = jnp.zeros((GROUP, 128), F32)
    for g in range(8):
        rows = min(GROUP, BLOCK - GROUP * g)
        part = dot(is_rel[GROUP * g : GROUP * g + GROUP, :], grads[...])
        for n in range(3):
            at = BLOCK * n + GROUP * g
            packed[at : at + rows, :] = part[:rows, 128 * n : 128 * n + 128]
        end = part[:, 384:]
        tail = tail + (pltpu.roll(end, LEFT * g, 1) if g else end)
    packed[3 * BLOCK : 3 * BLOCK + GROUP, :] = tail
    packed[3 * BLOCK + GROUP :, :] = jnp.zeros((PACKED - 3 * BLOCK - GROUP, 128), F32)
    t0[...] = packed[...].reshape(256, 16, 128).astype(BF16)

    remote(t0.at[pl.ds((1 - c) * 128, 128)], r0, sum_send.at[0], sum_recv.at[0], other).start()
    await_bytes(r0, sum_recv.at[0])
    t1[...] = (t0[pl.ds(c * 128, 128)].astype(F32) + r0[...].astype(F32)).astype(BF16)

    for step in range(1, 4):
        to_x, to_y = (x + step) % 4, (y + step) % 4
        remote(t1.at[pl.ds(16 * to_x, 16)], ra.at[0, x], sum_send.at[1], sum_recv.at[1], at_x(to_x)).start()
        remote(t1.at[pl.ds(64 + 16 * to_y, 16)], ra.at[1, y], sum_send.at[2], sum_recv.at[2], at_y(to_y)).start()
    ra[0, x] = t1[pl.ds(16 * x, 16)]
    ra[1, y] = t1[pl.ds(64 + 16 * y, 16)]

    def added(ref, lead, count):
        total = ref[lead + (0,)].astype(F32)
        for n in range(1, count):
            total = total + ref[lead + (n,)].astype(F32)
        return total.astype(BF16)

    await_bytes(ra.at[0, pl.ds(0, 3)], sum_recv.at[1])
    t2[0] = added(ra, (0,), 4)
    for step in range(1, 4):
        to_y = (y + step) % 4
        remote(t2.at[0, pl.ds(4 * to_y, 4)], rb.at[0, y], sum_send.at[3], sum_recv.at[3], at_y(to_y)).start()
    rb[0, y] = t2[0, pl.ds(4 * y, 4)]
    await_bytes(ra.at[1, pl.ds(0, 3)], sum_recv.at[2])
    t2[1] = added(ra, (1,), 4)
    for step in range(1, 4):
        to_x = (x + step) % 4
        remote(t2.at[1, pl.ds(4 * to_x, 4)], rb.at[1, x], sum_send.at[4], sum_recv.at[4], at_x(to_x)).start()
    rb[1, x] = t2[1, pl.ds(4 * x, 4)]
    await_bytes(rb.at[0, pl.ds(0, 3)], sum_recv.at[3])
    t3[0:4] = added(rb, (0,), 4)
    await_bytes(rb.at[1, pl.ds(0, 3)], sum_recv.at[4])
    t3[4:8] = added(rb, (1,), 4)

    def spread_z(step, _):
        to = (z + step) % 8
        remote(t3.at[to], rz.at[z], sum_send.at[5], sum_recv.at[5], at_z(to)).start()
        return 0

    lax.fori_loop(1, 8, spread_z, 0)
    rz[z] = t3[z]
    await_bytes(rz.at[pl.ds(0, 7)], sum_recv.at[5])

    which = z // 4
    base_x = c * 128 + 16 * x + 4 * y
    base_y = c * 128 + 64 + 16 * y + 4 * x
    spot = (1 - which) * base_x + which * base_y + z % 4
    gathered[spot] = added(rz, (), 8)

    def gather_z(step, _):
        to = (z + step) % 8
        remote(gathered.at[spot], gathered.at[spot], sum_send.at[6], sum_recv.at[6], at_z(to)).start()
        return 0

    lax.fori_loop(1, 8, gather_z, 0)
    await_bytes(gathered.at[pl.ds(0, 7)], sum_recv.at[6])

    def whole(first, count, n, device):
        part = gathered.at[pl.ds(first, count)]
        return remote(part, part, sum_send.at[n], sum_recv.at[n], device)

    for step in range(1, 4):
        to_x, to_y = (x + step) % 4, (y + step) % 4
        whole(base_x, 4, 7, at_y(to_y)).start()
        whole(base_y, 4, 8, at_x(to_x)).start()
    await_bytes(gathered.at[pl.ds(0, 12)], sum_recv.at[7])
    await_bytes(gathered.at[pl.ds(0, 12)], sum_recv.at[8])
    for step in range(1, 4):
        to_x, to_y = (x + step) % 4, (y + step) % 4
        whole(c * 128 + 16 * x, 16, 9, at_x(to_x)).start()
        whole(c * 128 + 64 + 16 * y, 16, 10, at_y(to_y)).start()
    await_bytes(gathered.at[pl.ds(0, 48)], sum_recv.at[9])
    await_bytes(gathered.at[pl.ds(0, 48)], sum_recv.at[10])
    whole(c * 128, 128, 11, other).start()
    emb_out[...] = emb[:, :D]
    state_out[...] = jnp.concatenate([as_row(state[:128]), as_row(state[128:])], axis=1)
    await_bytes(gathered.at[pl.ds(0, 128)], sum_recv.at[11])

    packed[...] = gathered[...].astype(F32).reshape(PACKED, 128)
    for g in range(8):
        rows = min(GROUP, NREL - GROUP * g)
        at = GROUP * g
        parts = [packed[BLOCK * n + at : BLOCK * n + at + rows, :] for n in range(3)]
        end = packed[3 * BLOCK : 3 * BLOCK + GROUP, :]
        end = (pltpu.roll(end, 128 - LEFT * g, 1) if g else end)[:rows, :LEFT]
        squares = parts[0] * parts[0] + parts[1] * parts[1] + parts[2] * parts[2]
        mean = jnp.sum(squares, axis=1, keepdims=True) + jnp.sum(end * end, axis=1, keepdims=True)
        fresh = state_col[at : at + rows, :] + mean * (1.0 / D)
        state_col[at : at + rows, :] = fresh
        root = jnp.sqrt(fresh)
        for n in range(3):
            cols = slice(128 * n, 128 * n + 128)
            rel_out[at : at + rows, cols] = relations[at : at + rows, cols] - learning_rate * parts[n] / root
        rel_out[at : at + rows, 384:] = relations[at : at + rows, 384:D] - learning_rate * end / root
    for n in range(11):
        width = min(128, NREL - 128 * n)
        row = as_row(state_col[128 * n : 128 * n + 128, :])
        rel_state_out[:, 128 * n : 128 * n + width] = row[:, :width]

    for r in range(ROUNDS):
        sent(r)
    await_bytes(t0.at[pl.ds(0, 128)], sum_send.at[0])
    for n, tiles in ((1, 48), (2, 48), (3, 12), (4, 12), (5, 7), (6, 7), (7, 12), (8, 12), (9, 48), (10, 48), (11, 128)):
        await_bytes(gathered.at[pl.ds(0, tiles)], sum_send.at[n])


def shards(
    embeddings,
    entity_state,
    relations,
    relation_state,
    round_masks,
    edge_src,
    edge_rel,
    edge_dst,
    edge_count,
    neg_rows,
):
    vmem = pl.BlockSpec(memory_space=pltpu.VMEM)

    def tiles(*lead):
        return pltpu.VMEM(lead + (16, 128), BF16)

    new_rows, new_state, new_relations, new_relation_state = pl.pallas_call(
        kernel,
        out_shape=(
            jax.ShapeDtypeStruct((ROWS, D), F32),
            jax.ShapeDtypeStruct((1, ROWS), F32),
            jax.ShapeDtypeStruct((NREL, D), F32),
            jax.ShapeDtypeStruct((1, NREL), F32),
        ),
        in_specs=[pl.BlockSpec(memory_space=pltpu.HBM)] * 10,
        out_specs=(vmem,) * 4,
        scratch_shapes=[
            pltpu.SMEM((ROUNDS,), jnp.int32),
            pltpu.SMEM((ROUNDS, EDGES), jnp.int32),
            pltpu.SMEM((ROUNDS, EDGES), jnp.int32),
            pltpu.SMEM((ROUNDS,), jnp.int32),
            pltpu.VMEM((D, ROWS), F32),
            pltpu.VMEM((1, ROWS), F32),
            pltpu.VMEM((D, NREL), F32),
            pltpu.VMEM((NREL,), F32),
            pltpu.VMEM((ROUNDS, EDGES), jnp.int32),
            pltpu.VMEM((ROUNDS, EDGES), jnp.int32),
            pltpu.VMEM((ROUNDS, EDGES), jnp.int32),
            pltpu.VMEM((ROUNDS, 1, NEG), jnp.int32),
            pltpu.VMEM((ROWS, WIDE), F32),
            pltpu.VMEM((REL_PAD, WIDE), F32),
            pltpu.VMEM((ROUNDS, EDGES, WIDE), F32),
            pltpu.VMEM((ROUNDS, EDGES, WIDE), F32),
            pltpu.VMEM((ROWS, WIDE), BF16),
            pltpu.VMEM((EDGES, WIDE), BF16),
            pltpu.VMEM((ROWS, WIDE), BF16),
            pltpu.VMEM((EDGES, WIDE), BF16),
            pltpu.VMEM((ROUNDS * EDGES, WIDE), BF16),
            pltpu.VMEM((8 * GROUP, ROUNDS * EDGES), BF16),
            pltpu.VMEM((PACKED, 128), F32),
            pltpu.VMEM((REL_PAD, 1), F32),
            tiles(ROUNDS, TILES),
            tiles(DEVICES),
            tiles(DEVICES),
            tiles(ROUNDS, DEVICES),
            tiles(ROUNDS, TILES),
            tiles(256),
            tiles(128),
            tiles(128),
            tiles(2, 4, 16),
            tiles(2, 16),
            tiles(2, 4, 4),
            tiles(8),
            tiles(8),
            tiles(256),
            pltpu.SemaphoreType.DMA((ROUNDS, 2)),
            pltpu.SemaphoreType.DMA((ROUNDS, 2)),
            pltpu.SemaphoreType.DMA((12,)),
            pltpu.SemaphoreType.DMA((12,)),
            pltpu.SemaphoreType.DMA((12,)),
        ],
        compiler_params=pltpu.CompilerParams(
            collective_id=0, has_side_effects=True, vmem_limit_bytes=60 * 1024 * 1024
        ),
    )(
        round_masks,
        edge_src,
        edge_rel,
        edge_count.reshape(ROUNDS),
        embeddings.T,
        entity_state.reshape(1, ROWS),
        relations.T,
        relation_state,
        edge_dst,
        neg_rows,
    )
    return (new_rows, new_state.reshape(ROWS), new_relations, new_relation_state.reshape(NREL))


def solution(mesh):
    placed = (
        P("dom", None),
        P("dom"),
        P(),
        P(),
        P(),
        P(None, "dom"),
        P(None, "dom"),
        P(None, "dom"),
        P(None, "dom"),
        P(None, "dom", None),
    )
    return jax.shard_map(
        shards,
        mesh=mesh,
        in_specs=placed,
        out_specs=(P("dom", None), P("dom"), P(), P()),
        check_vma=False,
    )
```

```python
import jax
import jax.numpy as jnp
from jax import lax
from jax.experimental import pallas as pl
from jax.experimental.pallas import tpu as pltpu
from jax.sharding import PartitionSpec as P

ROUNDS = 2
D = 400
NREL = 1300
NEG = 1000
ROWS = 256
EDGES = 128
WIDE = 512
LEFT = D - 384
CHIPS = 128
TILES = 76
REL_PAD = 1408
BLOCK = 1304
GROUP = 168
PACKED = 4096

learning_rate = 0.1

F32 = jnp.float32
BF16 = jnp.bfloat16


def iota(shape, dim):
    return lax.broadcasted_iota(jnp.int32, shape, dim)


def dot(a, b, left=1, right=0):
    return lax.dot_general(a, b, (((left,), (right,)), ((), ())), preferred_element_type=F32)


def halves(value):
    high = value.astype(BF16)
    return high, (value - high.astype(F32)).astype(BF16)


def as_column(row):
    count = row.shape[1]
    square = (count, count)
    return jnp.sum(jnp.where(iota(square, 0) == iota(square, 1), row, 0.0), axis=1, keepdims=True)


def as_row(column):
    count = column.shape[0]
    square = (count, count)
    return jnp.sum(jnp.where(iota(square, 0) == iota(square, 1), column, 0.0), axis=0, keepdims=True)


def remote(source, target, send, recv, device):
    return pltpu.make_async_remote_copy(
        src_ref=source,
        dst_ref=target,
        send_sem=send,
        recv_sem=recv,
        device_id=(device,),
        device_id_type=pl.DeviceIdType.MESH,
    )


def await_bytes(ref, sem):
    pltpu.make_async_copy(ref, ref, sem).wait()


def ring(offset):
    return min(offset, 4 - offset)


OFFSETS = sorted(
    ((dx, dy) for dx in range(4) for dy in range(4)),
    key=lambda offset: -ring(offset[0]) - ring(offset[1]),
)


def carrier(tile):
    return (5 * tile) // 3


def kernel(
    masks_hbm,
    src_hbm,
    rel_hbm,
    counts_hbm,
    emb_hbm,
    state_hbm,
    relations_hbm,
    rel_state_hbm,
    dst_hbm,
    neg_hbm,
    emb_out,
    state_out,
    rel_out,
    rel_state_out,
    masks,
    src_ids,
    rel_ids,
    counts,
    emb_in,
    state_in,
    rel_in,
    rel_state_in,
    src_rows,
    rel_rows,
    dst_rows,
    neg_rows,
    emb,
    relations,
    srcs,
    rels,
    table,
    vec,
    far_table,
    far_vec,
    grads,
    is_rel,
    packed,
    state_col,
    x1,
    held_0,
    held_1,
    x2,
    arrived_0,
    arrived_1,
    t0,
    r0,
    t1,
    ra,
    t3,
    rz,
    gathered,
    send,
    recv,
    sum_send,
    sum_recv,
    core_send,
    core_recv,
    gather_send,
    gather_recv,
    loaded,
):
    loads = [
        pltpu.make_async_copy(source, target, loaded.at[n])
        for n, (source, target) in enumerate(
            (
                (emb_hbm, emb_in),
                (relations_hbm, rel_in),
                (src_hbm, src_ids),
                (rel_hbm, rel_ids),
                (masks_hbm, masks),
                (counts_hbm, counts),
                (state_hbm, state_in),
                (rel_state_hbm, rel_state_in),
                (src_hbm, src_rows),
                (rel_hbm, rel_rows),
                (dst_hbm, dst_rows),
                (neg_hbm, neg_rows),
            )
        )
    ]
    for load in loads:
        load.start()
    me = lax.axis_index("dom")
    c = me % 2
    y = (me // 2) % 4
    x = (me // 8) % 4
    z = me // 32
    chip = me // 2
    mine = (3 * chip + 2) // 5
    active = jnp.logical_and(carrier(mine) == chip, mine < TILES)
    idle = jnp.logical_not(active)

    def plane(step):
        return (z + 4 + ((step + 1) // 2) * (1 - 2 * (step % 2))) % 8

    def first_tile(at):
        return (48 * at + 4) // 5

    def over_tiles(go):
        def one_plane(step, _):
            at = plane(step)
            lax.fori_loop(first_tile(at), jnp.minimum(first_tile(at + 1), TILES), go, 0)
            return 0

        lax.fori_loop(0, 8, one_plane, 0)

    places = [((x + dx) % 4) * 4 + (y + dy) % 4 for dx, dy in OFFSETS]
    place = places[-1]

    def at_place(to):
        return (z * 16 + to) * 2 + c

    def at_z(to):
        return (to * 16 + place) * 2 + c

    other = me + 1 - 2 * c

    barrier = pltpu.get_barrier_semaphore()

    def tell(device):
        pl.semaphore_signal(barrier, inc=1, device_id=(device,), device_id_type=pl.DeviceIdType.MESH)

    def tell_all(step, _):
        def tell_chip(n, _):
            to = 16 * plane(step) + n

            @pl.when(to != chip)
            def _():
                tell(2 * to + c)

            return 0

        lax.fori_loop(0, 16, tell_chip, 0)
        return 0

    def tell_carrier(i, _):
        tell(2 * carrier(i) + c)
        return 0

    @pl.when(active)
    def _():
        lax.fori_loop(0, 8, tell_all, 0)

    @pl.when(idle)
    def _():
        over_tiles(tell_carrier)

    for to in places[:-1]:
        tell(at_place(to))
    for step in range(7):
        tell(at_z(plane(step)))
    tell(other)

    def gather_rels(r):
        for e in range(EDGES):
            rels[r, e : e + 1, :] = relations[pl.ds(rel_ids[r, e], 1), :]

    def gather_srcs(r):
        for e in range(EDGES):
            srcs[r, e : e + 1, :] = emb[pl.ds(src_ids[r, e], 1), :]

    def hit_row(r):
        hits = jnp.sum((iota((ROWS, NEG), 0) == neg_rows[r]).astype(F32), axis=1, keepdims=True)
        return jnp.concatenate([as_row(hits[:128]), as_row(hits[128:])], axis=1)

    def bucket_rows(r):
        dst = dst_rows[r : r + 1, :].astype(F32)
        live = (iota((1, EDGES), 1) < counts[r]).astype(F32)
        return dst, live, hit_row(r)

    def pack(r, first, rows):
        for i in range(8):
            for j in range(3):
                x1[r, first + 3 * i + j] = rows[16 * i : 16 * i + 16, 128 * j : 128 * j + 128]
        last = rows[:, 384:].astype(F32)
        tail = last[:16]
        for g in range(1, 8):
            tail = tail + pltpu.roll(last[16 * g : 16 * g + 16], LEFT * g, 1)
        x1[r, first + 24] = tail.astype(BF16)

    def unpack(arrived, side, first, target, at):
        for i in range(8):
            for j in range(3):
                target[at + 16 * i : at + 16 * i + 16, 128 * j : 128 * j + 128] = arrived[side, first + 3 * i + j]
        tail = arrived[side, first + 24].astype(F32)
        inside = iota((16, 128), 1) < LEFT
        for g in range(8):
            part = pltpu.roll(tail, 128 - LEFT * g, 1) if g else tail
            target[at + 16 * g : at + 16 * g + 16, 384:] = jnp.where(inside, part, 0.0).astype(BF16)

    def pack_table(r):
        table[...] = emb[...].astype(BF16)
        pack(r, 0, table[0:128, :])
        pack(r, 25, table[128:256, :])

    def pack_vectors(r, rows):
        dst, live, hits = rows
        vec[...] = (srcs[r] * rels[r]).astype(BF16)
        pack(r, 50, vec[...])
        high = jnp.floor(hits * (1.0 / 16.0))
        low = hits - 16.0 * high
        extras = (dst, live, high[:, :128], high[:, 128:], low[:, :128], low[:, 128:])
        sub = iota((16, 128), 0)
        meta = jnp.zeros((16, 128), F32)
        for n, extra in enumerate(extras):
            meta = jnp.where(sub == n, extra, meta)
        x1[r, 75] = meta.astype(BF16)

    def exchange(r, mask, during):
        held = (held_0, held_1)[r]
        arrived = (arrived_0, arrived_1)[r]
        chip_mask = lax.shift_right_logical(mask, 1)
        side = lax.bitwise_and(mask, 1)

        def outward(i, _):
            to = carrier(i)

            @pl.when(to != chip)
            def _():
                remote(x1.at[r, i], held.at[chip], send.at[r, 0], recv.at[r, 0], 2 * to + c).start()

            @pl.when(to == chip)
            def _():
                held[chip] = x1[r, i]

            return 0

        over_tiles(outward)
        during()

        @pl.when(active)
        def _():
            await_bytes(held.at[pl.ds(0, CHIPS - 1)], recv.at[r, 0])

            def onward(step, _):
                base = 16 * plane(step)
                for n in range(16):
                    x2[r, base + n] = held[lax.bitwise_xor(chip_mask, base + n)]
                for n in places:
                    to = base + n

                    @pl.when(to != chip)
                    def _():
                        remote(x2.at[r, to], arrived.at[0, mine], send.at[r, 1], recv.at[r, 1], 2 * to + c).start()

                return 0

            lax.fori_loop(0, 8, onward, 0)
            arrived[0, mine] = x2[r, chip]
            await_bytes(arrived.at[0, pl.ds(0, TILES - 1)], recv.at[r, 1])

        @pl.when(idle)
        def _():
            await_bytes(arrived.at[0], recv.at[r, 1])

        remote(arrived.at[0], arrived.at[1], send.at[r, 2], recv.at[r, 2], other).start()
        await_bytes(arrived.at[1], recv.at[r, 2])

        unpack(arrived, side, 0, far_table, 0)
        unpack(arrived, side, 25, far_table, 128)
        unpack(arrived, side, 50, far_vec, 0)
        return arrived[side, 75].astype(F32)

    def sent(r):
        @pl.when(active)
        def _():
            await_bytes(x1.at[r, pl.ds(0, TILES - 1)], send.at[r, 0])
            await_bytes(x2.at[r, pl.ds(0, CHIPS - 1)], send.at[r, 1])

        @pl.when(idle)
        def _():
            await_bytes(x1.at[r], send.at[r, 0])

        await_bytes(x1.at[r], send.at[r, 2])

    def coefficients(vectors, rows, ends):
        dst, live, hits = ends
        scores = dot(vectors, rows, 1, 1)
        dst = as_column(dst)
        live = as_column(live)
        is_dst = iota((EDGES, ROWS), 1).astype(F32) == dst
        neg_coef = (live * (1.0 / (1.0 + jnp.exp(-scores))) / NEG).astype(BF16).astype(F32)
        positive = jnp.sum(jnp.where(is_dst, scores, 0.0), axis=1, keepdims=True)
        pos_coef = -live * (1.0 / (1.0 + jnp.exp(positive)))
        return halves(neg_coef * hits + jnp.where(is_dst, pos_coef, 0.0))

    for load in loads:
        load.wait()
    emb[:, 384:] = jnp.zeros((ROWS, 128), F32)
    for j in range(4):
        depth = min(128, D - 128 * j)
        for i in range(2):
            emb[128 * i : 128 * i + 128, 128 * j : 128 * j + depth] = emb_in[
                128 * j : 128 * j + depth, 128 * i : 128 * i + 128
            ].T
    pack_table(0)
    relations[:, 384:] = jnp.zeros((REL_PAD, 128), F32)
    for j in range(4):
        depth = min(128, D - 128 * j)
        for i in range(11):
            width = min(128, NREL - 128 * i)
            part = rel_in[128 * j : 128 * j + depth, 128 * i : 128 * i + width]
            if width < 128:
                part = jnp.concatenate([part, jnp.ones((depth, 128 - width), F32)], axis=1)
            relations[128 * i : 128 * i + 128, 128 * j : 128 * j + depth] = part.T
    gather_rels(0)
    gather_srcs(0)
    near = bucket_rows(0)
    pack_vectors(0, near)
    state = jnp.concatenate([as_column(state_in[:, :128]), as_column(state_in[:, 128:])], axis=0)

    @pl.when(active)
    def _():
        pl.semaphore_wait(barrier, CHIPS - 1 + 23)

    @pl.when(idle)
    def _():
        pl.semaphore_wait(barrier, TILES + 23)

    def prepare():
        gather_rels(1)
        later.append(bucket_rows(1))
        for n in range(11):
            width = min(128, NREL - 128 * n)
            part = rel_state_in[128 * n : 128 * n + width].reshape(1, width)
            if width < 128:
                part = jnp.concatenate([part, jnp.ones((1, 128 - width), F32)], axis=1)
            state_col[128 * n : 128 * n + 128, :] = as_column(part)

    def prepare_sum():
        ids = jnp.concatenate([rel_rows[0:1, :], rel_rows[1:2, :]], axis=1)
        for g in range(8):
            at = GROUP * g
            is_rel[at : at + GROUP, :] = (iota((GROUP, ROUNDS * EDGES), 0) + at == ids).astype(BF16)

    later = []
    for r in range(ROUNDS):
        meta = exchange(r, masks[r], prepare if r == 0 else prepare_sum)
        hits = jnp.concatenate([16.0 * meta[n : n + 1] + meta[n + 2 : n + 3] for n in (2, 3)], axis=1)
        far = (meta[0:1], meta[1:2], hits)

        high, low = coefficients(vec[...], far_table[...], near)
        pulled = (dot(high, far_table[...]) + dot(low, far_table[...])).astype(BF16).astype(F32)
        high, low = coefficients(far_vec[...], table[...], far)
        pushed = (dot(high, far_vec[...], 0, 0) + dot(low, far_vec[...], 0, 0)).astype(BF16).astype(F32)

        grads[r * EDGES : (r + 1) * EDGES, :] = (pulled * srcs[r]).astype(BF16)
        is_src = (iota((ROWS, EDGES), 0) == src_rows[r : r + 1, :]).astype(BF16)
        high, low = halves(pulled * rels[r])
        grad = pushed + dot(is_src, high) + dot(is_src, low)
        state = state + jnp.sum(grad * grad, axis=1, keepdims=True) * (1.0 / D)
        emb[...] = emb[...] - learning_rate * grad / jnp.sqrt(state)
        if r + 1 < ROUNDS:
            pack_table(r + 1)
            gather_srcs(r + 1)
            near = later[r]
            pack_vectors(r + 1, near)

    tail = jnp.zeros((GROUP, 128), F32)
    for g in range(8):
        rows = min(GROUP, BLOCK - GROUP * g)
        part = dot(is_rel[GROUP * g : GROUP * g + GROUP, :], grads[...])
        for n in range(3):
            at = BLOCK * n + GROUP * g
            packed[at : at + rows, :] = part[:rows, 128 * n : 128 * n + 128]
        end = part[:, 384:]
        tail = tail + (pltpu.roll(end, LEFT * g, 1) if g else end)
    packed[3 * BLOCK : 3 * BLOCK + GROUP, :] = tail
    packed[3 * BLOCK + GROUP :, :] = jnp.zeros((PACKED - 3 * BLOCK - GROUP, 128), F32)
    t0[...] = packed[...].reshape(256, 16, 128).astype(BF16)

    for k, to in enumerate(places):
        piece = pl.ds((1 - c) * 128 + 8 * to, 8)
        remote(t0.at[piece], r0.at[pl.ds(8 * to, 8)], core_send.at[k], core_recv.at[k], other).start()
    for k, to in enumerate(places):
        piece = pl.ds(8 * to, 8)
        await_bytes(r0.at[piece], core_recv.at[k])
        t1[piece] = (t0[pl.ds(c * 128 + 8 * to, 8)].astype(F32) + r0[piece].astype(F32)).astype(BF16)
        if k < 15:
            remote(t1.at[piece], ra.at[place], sum_send.at[0], sum_recv.at[0], at_place(to)).start()
    ra[place] = t1[pl.ds(8 * place, 8)]
    await_bytes(ra.at[pl.ds(0, 15)], sum_recv.at[0])

    def added(ref, count):
        total = ref[0].astype(F32)
        for n in range(1, count):
            total = total + ref[n].astype(F32)
        return total.astype(BF16)

    t3[...] = added(ra, 16)
    for step in range(7):
        to = plane(step)
        remote(t3.at[to], rz.at[z], sum_send.at[1], sum_recv.at[1], at_z(to)).start()
    rz[z] = t3[z]
    await_bytes(rz.at[pl.ds(0, 7)], sum_recv.at[1])

    base = c * 128 + 8 * place
    spot = base + z
    gathered[spot] = added(rz, 8)
    for step in range(7):
        to = plane(step)
        remote(gathered.at[spot], gathered.at[spot], sum_send.at[2], sum_recv.at[2], at_z(to)).start()
    await_bytes(gathered.at[pl.ds(0, 7)], sum_recv.at[2])

    own = gathered.at[pl.ds(base, 8)]
    for k, to in enumerate(places[:-1]):
        dx, dy = OFFSETS[k]
        back = OFFSETS.index((-dx % 4, -dy % 4))
        remote(own, own, gather_send.at[k], gather_recv.at[back], at_place(to)).start()
    for k, to in [(15, place)] + list(enumerate(places[:-1])):
        piece = gathered.at[pl.ds(c * 128 + 8 * to, 8)]
        if k < 15:
            await_bytes(piece, gather_recv.at[k])
        remote(piece, piece, sum_send.at[3], sum_recv.at[3], other).start()
    emb_out[...] = emb[:, :D]
    state_out[...] = jnp.concatenate([as_row(state[:128]), as_row(state[128:])], axis=1)
    await_bytes(gathered.at[pl.ds(0, 128)], sum_recv.at[3])

    packed[...] = gathered[...].astype(F32).reshape(PACKED, 128)
    for g in range(8):
        rows = min(GROUP, NREL - GROUP * g)
        at = GROUP * g
        parts = [packed[BLOCK * n + at : BLOCK * n + at + rows, :] for n in range(3)]
        end = packed[3 * BLOCK : 3 * BLOCK + GROUP, :]
        end = (pltpu.roll(end, 128 - LEFT * g, 1) if g else end)[:rows, :LEFT]
        squares = parts[0] * parts[0] + parts[1] * parts[1] + parts[2] * parts[2]
        mean = jnp.sum(squares, axis=1, keepdims=True) + jnp.sum(end * end, axis=1, keepdims=True)
        fresh = state_col[at : at + rows, :] + mean * (1.0 / D)
        state_col[at : at + rows, :] = fresh
        root = jnp.sqrt(fresh)
        for n in range(3):
            cols = slice(128 * n, 128 * n + 128)
            rel_out[at : at + rows, cols] = relations[at : at + rows, cols] - learning_rate * parts[n] / root
        rel_out[at : at + rows, 384:] = relations[at : at + rows, 384:D] - learning_rate * end / root
    for n in range(11):
        width = min(128, NREL - 128 * n)
        row = as_row(state_col[128 * n : 128 * n + 128, :])
        rel_state_out[:, 128 * n : 128 * n + width] = row[:, :width]

    for r in range(ROUNDS):
        sent(r)
    for k in range(16):
        await_bytes(r0.at[pl.ds(0, 8)], core_send.at[k])
    for n, tiles in ((0, 120), (1, 7), (2, 7), (3, 128)):
        await_bytes(gathered.at[pl.ds(0, tiles)], sum_send.at[n])
    for k in range(15):
        await_bytes(gathered.at[pl.ds(0, 8)], gather_send.at[k])


def shards(
    embeddings,
    entity_state,
    relations,
    relation_state,
    round_masks,
    edge_src,
    edge_rel,
    edge_dst,
    edge_count,
    neg_rows,
):
    vmem = pl.BlockSpec(memory_space=pltpu.VMEM)

    def tiles(*lead):
        return pltpu.VMEM(lead + (16, 128), BF16)

    new_rows, new_state, new_relations, new_relation_state = pl.pallas_call(
        kernel,
        out_shape=(
            jax.ShapeDtypeStruct((ROWS, D), F32),
            jax.ShapeDtypeStruct((1, ROWS), F32),
            jax.ShapeDtypeStruct((NREL, D), F32),
            jax.ShapeDtypeStruct((1, NREL), F32),
        ),
        in_specs=[pl.BlockSpec(memory_space=pltpu.HBM)] * 10,
        out_specs=(vmem,) * 4,
        scratch_shapes=[
            pltpu.SMEM((ROUNDS,), jnp.int32),
            pltpu.SMEM((ROUNDS, EDGES), jnp.int32),
            pltpu.SMEM((ROUNDS, EDGES), jnp.int32),
            pltpu.SMEM((ROUNDS,), jnp.int32),
            pltpu.VMEM((D, ROWS), F32),
            pltpu.VMEM((1, ROWS), F32),
            pltpu.VMEM((D, NREL), F32),
            pltpu.VMEM((NREL,), F32),
            pltpu.VMEM((ROUNDS, EDGES), jnp.int32),
            pltpu.VMEM((ROUNDS, EDGES), jnp.int32),
            pltpu.VMEM((ROUNDS, EDGES), jnp.int32),
            pltpu.VMEM((ROUNDS, 1, NEG), jnp.int32),
            pltpu.VMEM((ROWS, WIDE), F32),
            pltpu.VMEM((REL_PAD, WIDE), F32),
            pltpu.VMEM((ROUNDS, EDGES, WIDE), F32),
            pltpu.VMEM((ROUNDS, EDGES, WIDE), F32),
            pltpu.VMEM((ROWS, WIDE), BF16),
            pltpu.VMEM((EDGES, WIDE), BF16),
            pltpu.VMEM((ROWS, WIDE), BF16),
            pltpu.VMEM((EDGES, WIDE), BF16),
            pltpu.VMEM((ROUNDS * EDGES, WIDE), BF16),
            pltpu.VMEM((8 * GROUP, ROUNDS * EDGES), BF16),
            pltpu.VMEM((PACKED, 128), F32),
            pltpu.VMEM((REL_PAD, 1), F32),
            tiles(ROUNDS, TILES),
            tiles(CHIPS),
            tiles(CHIPS),
            tiles(ROUNDS, CHIPS),
            tiles(2, TILES),
            tiles(2, TILES),
            tiles(256),
            tiles(128),
            tiles(128),
            tiles(16, 8),
            tiles(8),
            tiles(8),
            tiles(256),
            pltpu.SemaphoreType.DMA((ROUNDS, 3)),
            pltpu.SemaphoreType.DMA((ROUNDS, 3)),
            pltpu.SemaphoreType.DMA((4,)),
            pltpu.SemaphoreType.DMA((4,)),
            pltpu.SemaphoreType.DMA((16,)),
            pltpu.SemaphoreType.DMA((16,)),
            pltpu.SemaphoreType.DMA((15,)),
            pltpu.SemaphoreType.DMA((15,)),
            pltpu.SemaphoreType.DMA((12,)),
        ],
        compiler_params=pltpu.CompilerParams(
            collective_id=0, has_side_effects=True, vmem_limit_bytes=60 * 1024 * 1024
        ),
    )(
        round_masks,
        edge_src,
        edge_rel,
        edge_count.reshape(ROUNDS),
        embeddings.T,
        entity_state.reshape(1, ROWS),
        relations.T,
        relation_state,
        edge_dst,
        neg_rows,
    )
    return (new_rows, new_state.reshape(ROWS), new_relations, new_relation_state.reshape(NREL))


def solution(mesh):
    placed = (
        P("dom", None),
        P("dom"),
        P(),
        P(),
        P(),
        P(None, "dom"),
        P(None, "dom"),
        P(None, "dom"),
        P(None, "dom"),
        P(None, "dom", None),
    )
    return jax.shard_map(
        shards,
        mesh=mesh,
        in_specs=placed,
        out_specs=(P("dom", None), P("dom"), P(), P()),
        check_vma=False,
    )
```

```python
import jax
import jax.numpy as jnp
from jax import lax
from jax.experimental import pallas as pl
from jax.experimental.pallas import tpu as pltpu
from jax.sharding import PartitionSpec as P

ROUNDS = 2
D = 400
NREL = 1300
NEG = 1000
ROWS = 256
EDGES = 128
WIDE = 512
LEFT = D - 384
CHIPS = 128
TILES = 76
ROW_TILES = 51
VEC_TILES = 25
REL_PAD = 1408
BLOCK = 1304
GROUP = 168
PACKED = 4096

learning_rate = 0.1

F32 = jnp.float32
BF16 = jnp.bfloat16


def iota(shape, dim):
    return lax.broadcasted_iota(jnp.int32, shape, dim)


def dot(a, b, left=1, right=0):
    return lax.dot_general(a, b, (((left,), (right,)), ((), ())), preferred_element_type=F32)


def halves(value):
    high = value.astype(BF16)
    return high, (value - high.astype(F32)).astype(BF16)


def as_column(row):
    count = row.shape[1]
    square = (count, count)
    return jnp.sum(jnp.where(iota(square, 0) == iota(square, 1), row, 0.0), axis=1, keepdims=True)


def as_row(column):
    count = column.shape[0]
    square = (count, count)
    return jnp.sum(jnp.where(iota(square, 0) == iota(square, 1), column, 0.0), axis=0, keepdims=True)


def remote(source, target, send, recv, device):
    return pltpu.make_async_remote_copy(
        src_ref=source,
        dst_ref=target,
        send_sem=send,
        recv_sem=recv,
        device_id=(device,),
        device_id_type=pl.DeviceIdType.MESH,
    )


def await_bytes(ref, sem):
    pltpu.make_async_copy(ref, ref, sem).wait()


def ring(offset):
    return min(offset, 4 - offset)


OFFSETS = sorted(
    ((dx, dy) for dx in range(4) for dy in range(4)),
    key=lambda offset: -ring(offset[0]) - ring(offset[1]),
)


def row_carrier(tile):
    return (5 * tile) // 2


def vec_carrier(tile):
    return 5 * (tile - ROW_TILES) + 1


def kernel(
    masks_hbm,
    src_hbm,
    rel_hbm,
    counts_hbm,
    emb_hbm,
    state_hbm,
    relations_hbm,
    dst_hbm,
    neg_hbm,
    emb_out,
    state_out,
    gathered,
    masks,
    src_ids,
    rel_ids,
    counts,
    emb_in,
    state_in,
    rel_in,
    src_rows,
    rel_rows,
    dst_rows,
    neg_rows,
    emb,
    relations,
    srcs,
    rels,
    table,
    vec,
    far_table,
    far_vec,
    grads,
    is_rel,
    packed,
    x1,
    held_0,
    held_1,
    x2,
    rows_0,
    rows_1,
    vecs_0,
    vecs_1,
    t0,
    r0,
    t1,
    ra,
    t3,
    rz,
    send,
    recv,
    sum_send,
    sum_recv,
    core_send,
    core_recv,
    gather_send,
    gather_recv,
    loaded,
):
    loads = [
        pltpu.make_async_copy(source, target, loaded.at[n])
        for n, (source, target) in enumerate(
            (
                (emb_hbm, emb_in),
                (relations_hbm, rel_in),
                (src_hbm, src_ids),
                (rel_hbm, rel_ids),
                (masks_hbm, masks),
                (counts_hbm, counts),
                (state_hbm, state_in),
                (src_hbm, src_rows),
                (rel_hbm, rel_rows),
                (dst_hbm, dst_rows),
                (neg_hbm, neg_rows),
            )
        )
    ]
    for load in loads:
        load.start()
    me = lax.axis_index("dom")
    c = me % 2
    y = (me // 2) % 4
    x = (me // 8) % 4
    z = me // 32
    chip = me // 2
    row_mine = (2 * chip + 1) // 5
    vec_mine = ROW_TILES + chip // 5
    has_row = jnp.logical_and(row_carrier(row_mine) == chip, row_mine < ROW_TILES)
    has_vec = jnp.logical_and(vec_carrier(vec_mine) == chip, vec_mine < TILES)
    active = jnp.logical_or(has_row, has_vec)
    idle = jnp.logical_not(active)

    def plane(step):
        return (z + 4 + ((step + 1) // 2) * (1 - 2 * (step % 2))) % 8

    def over_rows(go):
        def first(at):
            return (32 * at + 4) // 5

        def one_plane(step, _):
            at = plane(step)

            def one(i, _):
                go(i, row_carrier(i))
                return 0

            lax.fori_loop(first(at), jnp.minimum(first(at + 1), ROW_TILES), one, 0)
            return 0

        lax.fori_loop(0, 8, one_plane, 0)

    def over_vecs(go):
        def first(at):
            return (16 * at + 3) // 5

        def one_plane(step, _):
            at = plane(step)

            def one(i, _):
                go(ROW_TILES + i, vec_carrier(ROW_TILES + i))
                return 0

            lax.fori_loop(first(at), jnp.minimum(first(at + 1), VEC_TILES), one, 0)
            return 0

        lax.fori_loop(0, 8, one_plane, 0)

    places = [((x + dx) % 4) * 4 + (y + dy) % 4 for dx, dy in OFFSETS]
    place = places[-1]

    def at_place(to):
        return (z * 16 + to) * 2 + c

    def at_z(to):
        return (to * 16 + place) * 2 + c

    other = me + 1 - 2 * c

    barrier = pltpu.get_barrier_semaphore()

    def tell(device):
        pl.semaphore_signal(barrier, inc=1, device_id=(device,), device_id_type=pl.DeviceIdType.MESH)

    def tell_all(step, _):
        def tell_chip(n, _):
            to = 16 * plane(step) + n

            @pl.when(to != chip)
            def _():
                tell(2 * to + c)

            return 0

        lax.fori_loop(0, 16, tell_chip, 0)
        return 0

    def tell_carrier(i, to):
        tell(2 * to + c)

    @pl.when(active)
    def _():
        lax.fori_loop(0, 8, tell_all, 0)

    @pl.when(idle)
    def _():
        over_rows(tell_carrier)
        over_vecs(tell_carrier)

    for to in places[:-1]:
        tell(at_place(to))
    for step in range(7):
        tell(at_z(plane(step)))
    tell(other)

    def gather_rels(r):
        for e in range(EDGES):
            rels[r, e : e + 1, :] = relations[pl.ds(rel_ids[r, e], 1), :]

    def gather_srcs(r):
        for e in range(EDGES):
            srcs[r, e : e + 1, :] = emb[pl.ds(src_ids[r, e], 1), :]

    def hit_row(r):
        hits = jnp.sum((iota((ROWS, NEG), 0) == neg_rows[r]).astype(F32), axis=1, keepdims=True)
        return jnp.concatenate([as_row(hits[:128]), as_row(hits[128:])], axis=1)

    def bucket_rows(r):
        dst = dst_rows[r : r + 1, :].astype(F32)
        live = (iota((1, EDGES), 1) < counts[r]).astype(F32)
        return dst, live, hit_row(r)

    def pack(r, first, rows):
        for i in range(8):
            for j in range(3):
                x1[r, first + 3 * i + j] = rows[16 * i : 16 * i + 16, 128 * j : 128 * j + 128]
        last = rows[:, 384:].astype(F32)
        tail = last[:16]
        for g in range(1, 8):
            tail = tail + pltpu.roll(last[16 * g : 16 * g + 16], LEFT * g, 1)
        x1[r, first + 24] = tail.astype(BF16)

    def unpack(arrived, side, first, target, at):
        for i in range(8):
            for j in range(3):
                target[at + 16 * i : at + 16 * i + 16, 128 * j : 128 * j + 128] = arrived[side, first + 3 * i + j]
        tail = arrived[side, first + 24].astype(F32)
        inside = iota((16, 128), 1) < LEFT
        for g in range(8):
            part = pltpu.roll(tail, 128 - LEFT * g, 1) if g else tail
            target[at + 16 * g : at + 16 * g + 16, 384:] = jnp.where(inside, part, 0.0).astype(BF16)

    def pack_table(r):
        table[...] = emb[...].astype(BF16)
        pack(r, 0, table[0:128, :])
        pack(r, 25, table[128:256, :])

    def pack_vectors(r):
        vec[...] = (srcs[r] * rels[r]).astype(BF16)
        pack(r, ROW_TILES, vec[...])

    def pack_meta(r, rows):
        dst, live, hits = rows
        high = jnp.floor(hits * (1.0 / 16.0))
        low = hits - 16.0 * high
        extras = (dst, live, high[:, :128], high[:, 128:], low[:, :128], low[:, 128:])
        sub = iota((16, 128), 0)
        meta = jnp.zeros((16, 128), F32)
        for n, extra in enumerate(extras):
            meta = jnp.where(sub == n, extra, meta)
        x1[r, 50] = meta.astype(BF16)

    def send_out(r, over):
        held = (held_0, held_1)[r]

        def outward(i, to):
            @pl.when(to != chip)
            def _():
                remote(x1.at[r, i], held.at[chip], send.at[r, 0], recv.at[r, 0], 2 * to + c).start()

            @pl.when(to == chip)
            def _():
                held[chip] = x1[r, i]

        over(outward)

    def relay(r, mask, arrived, mine, sem):
        held = (held_0, held_1)[r]
        chip_mask = lax.shift_right_logical(mask, 1)
        await_bytes(held.at[pl.ds(0, CHIPS - 1)], recv.at[r, 0])

        def onward(step, _):
            base = 16 * plane(step)
            for n in range(16):
                x2[r, base + n] = held[lax.bitwise_xor(chip_mask, base + n)]
            for n in places:
                to = base + n

                @pl.when(to != chip)
                def _():
                    remote(x2.at[r, to], arrived.at[0, mine], send.at[r, 1], recv.at[r, sem], 2 * to + c).start()

            return 0

        lax.fori_loop(0, 8, onward, 0)
        arrived[0, mine] = x2[r, chip]

    def take_in(r, has, arrived, count, sem):
        @pl.when(has)
        def _():
            await_bytes(arrived.at[0, pl.ds(0, count - 1)], recv.at[r, sem])

        @pl.when(jnp.logical_not(has))
        def _():
            await_bytes(arrived.at[0], recv.at[r, sem])

        remote(arrived.at[0], arrived.at[1], send.at[r, sem + 1], recv.at[r, sem + 1], other).start()
        await_bytes(arrived.at[1], recv.at[r, sem + 1])

    def sent(r):
        @pl.when(active)
        def _():
            await_bytes(x1.at[r, pl.ds(0, TILES - 1)], send.at[r, 0])
            await_bytes(x2.at[r, pl.ds(0, CHIPS - 1)], send.at[r, 1])

        @pl.when(idle)
        def _():
            await_bytes(x1.at[r], send.at[r, 0])

        await_bytes(x1.at[r, pl.ds(0, ROW_TILES)], send.at[r, 2])
        await_bytes(x1.at[r, pl.ds(0, VEC_TILES)], send.at[r, 4])

    def coefficients(vectors, rows, ends):
        dst, live, hits = ends
        scores = dot(vectors, rows, 1, 1)
        dst = as_column(dst)
        live = as_column(live)
        is_dst = iota((EDGES, ROWS), 1).astype(F32) == dst
        neg_coef = (live * (1.0 / (1.0 + jnp.exp(-scores))) / NEG).astype(BF16).astype(F32)
        positive = jnp.sum(jnp.where(is_dst, scores, 0.0), axis=1, keepdims=True)
        pos_coef = -live * (1.0 / (1.0 + jnp.exp(positive)))
        return halves(neg_coef * hits + jnp.where(is_dst, pos_coef, 0.0))

    for load in loads:
        load.wait()
    emb[:, 384:] = jnp.zeros((ROWS, 128), F32)
    for j in range(4):
        depth = min(128, D - 128 * j)
        for i in range(2):
            emb[128 * i : 128 * i + 128, 128 * j : 128 * j + depth] = emb_in[
                128 * j : 128 * j + depth, 128 * i : 128 * i + 128
            ].T
    pack_table(0)
    buckets = [bucket_rows(r) for r in range(ROUNDS)]
    for r in range(ROUNDS):
        pack_meta(r, buckets[r])
    state = jnp.concatenate([as_column(state_in[:, :128]), as_column(state_in[:, 128:])], axis=0)

    gather_srcs(0)
    relations[:, 384:] = jnp.zeros((REL_PAD, 128), F32)
    for j in range(4):
        depth = min(128, D - 128 * j)
        for i in range(11):
            width = min(128, NREL - 128 * i)
            part = rel_in[128 * j : 128 * j + depth, 128 * i : 128 * i + width]
            if width < 128:
                part = jnp.concatenate([part, jnp.ones((depth, 128 - width), F32)], axis=1)
            relations[128 * i : 128 * i + 128, 128 * j : 128 * j + depth] = part.T
    for r in range(ROUNDS):
        gather_rels(r)
    pack_vectors(0)

    @pl.when(active)
    def _():
        pl.semaphore_wait(barrier, CHIPS - 1 + 23)

    @pl.when(idle)
    def _():
        pl.semaphore_wait(barrier, TILES + 23)

    def prepare_sum():
        ids = jnp.concatenate([rel_rows[0:1, :], rel_rows[1:2, :]], axis=1)
        for g in range(8):
            at = GROUP * g
            is_rel[at : at + GROUP, :] = (iota((GROUP, ROUNDS * EDGES), 0) + at == ids).astype(BF16)

    for r in range(ROUNDS):
        mask = masks[r]
        side = lax.bitwise_and(mask, 1)
        far_rows = (rows_0, rows_1)[r]
        far_vecs = (vecs_0, vecs_1)[r]
        send_out(r, over_rows)
        if r > 0:
            gather_srcs(r)
            pack_vectors(r)
        send_out(r, over_vecs)
        if r == 0:
            prepare_sum()

        @pl.when(has_row)
        def _():
            relay(r, mask, far_rows, row_mine, 1)

        @pl.when(has_vec)
        def _():
            relay(r, mask, far_vecs, vec_mine - ROW_TILES, 3)

        take_in(r, has_row, far_rows, ROW_TILES, 1)
        unpack(far_rows, side, 0, far_table, 0)
        unpack(far_rows, side, 25, far_table, 128)
        meta = far_rows[side, 50].astype(F32)
        hits = jnp.concatenate([16.0 * meta[n : n + 1] + meta[n + 2 : n + 3] for n in (2, 3)], axis=1)
        far = (meta[0:1], meta[1:2], hits)

        high, low = coefficients(vec[...], far_table[...], buckets[r])
        pulled = (dot(high, far_table[...]) + dot(low, far_table[...])).astype(BF16).astype(F32)
        take_in(r, has_vec, far_vecs, VEC_TILES, 3)
        unpack(far_vecs, side, 0, far_vec, 0)
        high, low = coefficients(far_vec[...], table[...], far)
        pushed = (dot(high, far_vec[...], 0, 0) + dot(low, far_vec[...], 0, 0)).astype(BF16).astype(F32)

        grads[r * EDGES : (r + 1) * EDGES, :] = (pulled * srcs[r]).astype(BF16)
        is_src = (iota((ROWS, EDGES), 0) == src_rows[r : r + 1, :]).astype(BF16)
        high, low = halves(pulled * rels[r])
        grad = pushed + dot(is_src, high) + dot(is_src, low)
        state = state + jnp.sum(grad * grad, axis=1, keepdims=True) * (1.0 / D)
        emb[...] = emb[...] - learning_rate * grad / jnp.sqrt(state)
        if r + 1 < ROUNDS:
            pack_table(r + 1)

    tail = jnp.zeros((GROUP, 128), F32)
    for g in range(8):
        rows = min(GROUP, BLOCK - GROUP * g)
        part = dot(is_rel[GROUP * g : GROUP * g + GROUP, :], grads[...])
        for n in range(3):
            at = BLOCK * n + GROUP * g
            packed[at : at + rows, :] = part[:rows, 128 * n : 128 * n + 128]
        end = part[:, 384:]
        tail = tail + (pltpu.roll(end, LEFT * g, 1) if g else end)
    packed[3 * BLOCK : 3 * BLOCK + GROUP, :] = tail
    packed[3 * BLOCK + GROUP :, :] = jnp.zeros((PACKED - 3 * BLOCK - GROUP, 128), F32)
    t0[...] = packed[...].reshape(256, 16, 128).astype(BF16)

    for k, to in enumerate(places):
        piece = pl.ds((1 - c) * 128 + 8 * to, 8)
        remote(t0.at[piece], r0.at[pl.ds(8 * to, 8)], core_send.at[k], core_recv.at[k], other).start()
    for k, to in enumerate(places):
        piece = pl.ds(8 * to, 8)
        await_bytes(r0.at[piece], core_recv.at[k])
        t1[piece] = (t0[pl.ds(c * 128 + 8 * to, 8)].astype(F32) + r0[piece].astype(F32)).astype(BF16)
        if k < 15:
            remote(t1.at[piece], ra.at[place], sum_send.at[0], sum_recv.at[0], at_place(to)).start()
    ra[place] = t1[pl.ds(8 * place, 8)]
    await_bytes(ra.at[pl.ds(0, 15)], sum_recv.at[0])

    def added(ref, count):
        total = ref[0].astype(F32)
        for n in range(1, count):
            total = total + ref[n].astype(F32)
        return total.astype(BF16)

    t3[...] = added(ra, 16)
    for step in range(7):
        to = plane(step)
        remote(t3.at[to], rz.at[z], sum_send.at[1], sum_recv.at[1], at_z(to)).start()
    rz[z] = t3[z]
    await_bytes(rz.at[pl.ds(0, 7)], sum_recv.at[1])

    base = c * 128 + 8 * place
    spot = base + z
    gathered[spot] = added(rz, 8)
    for step in range(7):
        to = plane(step)
        remote(gathered.at[spot], gathered.at[spot], sum_send.at[2], sum_recv.at[2], at_z(to)).start()
    await_bytes(gathered.at[pl.ds(0, 7)], sum_recv.at[2])

    own = gathered.at[pl.ds(base, 8)]
    for k, to in enumerate(places[:-1]):
        dx, dy = OFFSETS[k]
        back = OFFSETS.index((-dx % 4, -dy % 4))
        remote(own, own, gather_send.at[k], gather_recv.at[back], at_place(to)).start()
    for k, to in [(15, place)] + list(enumerate(places[:-1])):
        piece = gathered.at[pl.ds(c * 128 + 8 * to, 8)]
        if k < 15:
            await_bytes(piece, gather_recv.at[k])
        remote(piece, piece, sum_send.at[3], sum_recv.at[3], other).start()
    for j in range(4):
        depth = min(128, D - 128 * j)
        for i in range(2):
            part = emb[128 * i : 128 * i + 128, 128 * j : 128 * j + 128].T
            emb_out[128 * j : 128 * j + depth, 128 * i : 128 * i + 128] = part[:depth]
    state_out[...] = jnp.concatenate([as_row(state[:128]), as_row(state[128:])], axis=1)
    await_bytes(gathered.at[pl.ds(0, 128)], sum_recv.at[3])

    for r in range(ROUNDS):
        sent(r)
    for k in range(16):
        await_bytes(r0.at[pl.ds(0, 8)], core_send.at[k])
    for n, tiles in ((0, 120), (1, 7), (2, 7), (3, 128)):
        await_bytes(gathered.at[pl.ds(0, tiles)], sum_send.at[n])
    for k in range(15):
        await_bytes(gathered.at[pl.ds(0, 8)], gather_send.at[k])


def finish(
    emb_hbm,
    state_hbm,
    sums_hbm,
    rel_hbm,
    rel_state_hbm,
    emb_out,
    state_out,
    rel_out,
    rel_state_out,
    sums,
    rel_in,
    state_in,
    rel_state_in,
    packed,
    tails,
    rel_new,
    state_new,
    rel_state_new,
    emb_kept,
    sems,
):
    loads = [
        pltpu.make_async_copy(sums_hbm, sums, sems.at[0]),
        pltpu.make_async_copy(rel_state_hbm, rel_state_in, sems.at[1]),
        pltpu.make_async_copy(rel_hbm, rel_in, sems.at[2]),
        pltpu.make_async_copy(state_hbm, state_in, sems.at[3]),
    ]
    loads.append(pltpu.make_async_copy(emb_hbm, emb_kept, sems.at[4]))
    for load in loads:
        load.start()
    for load in loads:
        load.wait()
    state_new[...] = state_in[...].reshape(ROWS)
    stores = [
        pltpu.make_async_copy(state_new, state_out, sems.at[5]),
        pltpu.make_async_copy(emb_kept, emb_out, sems.at[8]),
    ]
    for store in stores:
        store.start()
    packed[...] = sums[...].astype(F32).reshape(PACKED, 128)
    end = packed[3 * BLOCK : 3 * BLOCK + GROUP, :]
    inside = iota((GROUP, 128), 1) < LEFT
    for g in range(8):
        part = pltpu.roll(end, 128 - LEFT * g, 1) if g else end
        tails[GROUP * g : GROUP * g + GROUP, :] = jnp.where(inside, part, 0.0)
    tails[8 * GROUP :, :] = jnp.zeros((REL_PAD - 8 * GROUP, 128), F32)
    for i in range(11):
        at = 128 * i
        width = min(128, NREL - at)
        rows = min(128, BLOCK - at)
        parts = [packed[BLOCK * n + at : BLOCK * n + at + rows, :] for n in range(3)] + [tails[at : at + rows, :]]
        if rows < 128:
            parts = [jnp.concatenate([part, jnp.zeros((128 - rows, 128), F32)], axis=0) for part in parts]
        old = rel_state_in[at : at + width].reshape(1, width)
        if width < 128:
            old = jnp.concatenate([old, jnp.ones((1, 128 - width), F32)], axis=1)
        squares = parts[0] * parts[0] + parts[1] * parts[1] + parts[2] * parts[2] + parts[3] * parts[3]
        fresh = old + as_row(jnp.sum(squares, axis=1, keepdims=True)) * (1.0 / D)
        rel_state_new[at : at + width] = fresh[:, :width].reshape(width)
        root = jnp.sqrt(fresh)
        for n in range(4):
            depth = min(128, D - 128 * n)
            change = learning_rate * parts[n].T[:depth] / root
            cols = slice(128 * n, 128 * n + depth)
            rel_new[cols, at : at + width] = rel_in[cols, at : at + width] - change[:, :width]
    stores.append(pltpu.make_async_copy(rel_new, rel_out, sems.at[6]))
    stores.append(pltpu.make_async_copy(rel_state_new, rel_state_out, sems.at[7]))
    for store in stores[2:]:
        store.start()
    for store in stores:
        store.wait()


def shards(
    embeddings,
    entity_state,
    relations,
    relation_state,
    round_masks,
    edge_src,
    edge_rel,
    edge_dst,
    edge_count,
    neg_rows,
):
    vmem = pl.BlockSpec(memory_space=pltpu.VMEM)

    def tiles(*lead):
        return pltpu.VMEM(lead + (16, 128), BF16)

    hbm = pl.BlockSpec(memory_space=pltpu.HBM)
    rows_t, state, sums = pl.pallas_call(
        kernel,
        out_shape=(
            jax.ShapeDtypeStruct((D, ROWS), F32),
            jax.ShapeDtypeStruct((1, ROWS), F32),
            jax.ShapeDtypeStruct((256, 16, 128), BF16),
        ),
        in_specs=[hbm] * 9,
        out_specs=(vmem,) * 3,
        scratch_shapes=[
            pltpu.SMEM((ROUNDS,), jnp.int32),
            pltpu.SMEM((ROUNDS, EDGES), jnp.int32),
            pltpu.SMEM((ROUNDS, EDGES), jnp.int32),
            pltpu.SMEM((ROUNDS,), jnp.int32),
            pltpu.VMEM((D, ROWS), F32),
            pltpu.VMEM((1, ROWS), F32),
            pltpu.VMEM((D, NREL), F32),
            pltpu.VMEM((ROUNDS, EDGES), jnp.int32),
            pltpu.VMEM((ROUNDS, EDGES), jnp.int32),
            pltpu.VMEM((ROUNDS, EDGES), jnp.int32),
            pltpu.VMEM((ROUNDS, 1, NEG), jnp.int32),
            pltpu.VMEM((ROWS, WIDE), F32),
            pltpu.VMEM((REL_PAD, WIDE), F32),
            pltpu.VMEM((ROUNDS, EDGES, WIDE), F32),
            pltpu.VMEM((ROUNDS, EDGES, WIDE), F32),
            pltpu.VMEM((ROWS, WIDE), BF16),
            pltpu.VMEM((EDGES, WIDE), BF16),
            pltpu.VMEM((ROWS, WIDE), BF16),
            pltpu.VMEM((EDGES, WIDE), BF16),
            pltpu.VMEM((ROUNDS * EDGES, WIDE), BF16),
            pltpu.VMEM((8 * GROUP, ROUNDS * EDGES), BF16),
            pltpu.VMEM((PACKED, 128), F32),
            tiles(ROUNDS, TILES),
            tiles(CHIPS),
            tiles(CHIPS),
            tiles(ROUNDS, CHIPS),
            tiles(2, ROW_TILES),
            tiles(2, ROW_TILES),
            tiles(2, VEC_TILES),
            tiles(2, VEC_TILES),
            tiles(256),
            tiles(128),
            tiles(128),
            tiles(16, 8),
            tiles(8),
            tiles(8),
            pltpu.SemaphoreType.DMA((ROUNDS, 5)),
            pltpu.SemaphoreType.DMA((ROUNDS, 5)),
            pltpu.SemaphoreType.DMA((4,)),
            pltpu.SemaphoreType.DMA((4,)),
            pltpu.SemaphoreType.DMA((16,)),
            pltpu.SemaphoreType.DMA((16,)),
            pltpu.SemaphoreType.DMA((15,)),
            pltpu.SemaphoreType.DMA((15,)),
            pltpu.SemaphoreType.DMA((12,)),
        ],
        compiler_params=pltpu.CompilerParams(
            collective_id=0, has_side_effects=True, vmem_limit_bytes=60 * 1024 * 1024
        ),
    )(
        round_masks,
        edge_src,
        edge_rel,
        edge_count.reshape(ROUNDS),
        embeddings.T,
        entity_state.reshape(1, ROWS),
        relations.T,
        edge_dst,
        neg_rows,
    )
    new_rows, new_state, new_relations, new_relation_state = pl.pallas_call(
        finish,
        out_shape=(
            jax.ShapeDtypeStruct((D, ROWS), F32),
            jax.ShapeDtypeStruct((ROWS,), F32),
            jax.ShapeDtypeStruct((D, NREL), F32),
            jax.ShapeDtypeStruct((NREL,), F32),
        ),
        in_specs=[hbm] * 5,
        out_specs=(hbm,) * 4,
        scratch_shapes=[
            tiles(256),
            pltpu.VMEM((D, NREL), F32),
            pltpu.VMEM((1, ROWS), F32),
            pltpu.VMEM((NREL,), F32),
            pltpu.VMEM((PACKED, 128), F32),
            pltpu.VMEM((REL_PAD, 128), F32),
            pltpu.VMEM((D, NREL), F32),
            pltpu.VMEM((ROWS,), F32),
            pltpu.VMEM((NREL,), F32),
            pltpu.VMEM((D, ROWS), F32),
            pltpu.SemaphoreType.DMA((9,)),
        ],
        compiler_params=pltpu.CompilerParams(vmem_limit_bytes=60 * 1024 * 1024),
    )(rows_t, state, sums, relations.T, relation_state)
    return (new_rows.T, new_state, new_relations.T, new_relation_state)


def solution(mesh):
    placed = (
        P("dom", None),
        P("dom"),
        P(),
        P(),
        P(),
        P(None, "dom"),
        P(None, "dom"),
        P(None, "dom"),
        P(None, "dom"),
        P(None, "dom", None),
    )
    return jax.shard_map(
        shards,
        mesh=mesh,
        in_specs=placed,
        out_specs=(P("dom", None), P("dom"), P(), P()),
        check_vma=False,
    )
```

```python
import jax
import jax.numpy as jnp
from jax import lax
from jax.experimental import pallas as pl
from jax.experimental.pallas import tpu as pltpu
from jax.sharding import PartitionSpec as P

ROUNDS = 2
D = 400
NREL = 1300
NEG = 1000
ROWS = 256
EDGES = 128
WIDE = 512
LEFT = D - 384
CHIPS = 128
TILES = 76
ROW_TILES = 51
VEC_TILES = 25
REL_PAD = 1408
BLOCK = 1304
GROUP = 168
PACKED = 4096

learning_rate = 0.1

F32 = jnp.float32
BF16 = jnp.bfloat16


def iota(shape, dim):
    return lax.broadcasted_iota(jnp.int32, shape, dim)


def dot(a, b, left=1, right=0):
    return lax.dot_general(a, b, (((left,), (right,)), ((), ())), preferred_element_type=F32)


def halves(value):
    high = value.astype(BF16)
    return high, (value - high.astype(F32)).astype(BF16)


def as_column(row):
    count = row.shape[1]
    square = (count, count)
    return jnp.sum(jnp.where(iota(square, 0) == iota(square, 1), row, 0.0), axis=1, keepdims=True)


def as_row(column):
    count = column.shape[0]
    square = (count, count)
    return jnp.sum(jnp.where(iota(square, 0) == iota(square, 1), column, 0.0), axis=0, keepdims=True)


def remote(source, target, send, recv, device):
    return pltpu.make_async_remote_copy(
        src_ref=source,
        dst_ref=target,
        send_sem=send,
        recv_sem=recv,
        device_id=(device,),
        device_id_type=pl.DeviceIdType.MESH,
    )


def await_bytes(ref, sem):
    pltpu.make_async_copy(ref, ref, sem).wait()


def ring(offset):
    return min(offset, 4 - offset)


OFFSETS = sorted(
    ((dx, dy) for dx in range(4) for dy in range(4)),
    key=lambda offset: -ring(offset[0]) - ring(offset[1]),
)


def row_carrier(tile):
    return (5 * tile) // 2


def vec_carrier(tile):
    return 5 * (tile - ROW_TILES) + 1


def kernel(
    masks_hbm,
    src_hbm,
    rel_hbm,
    counts_hbm,
    emb_hbm,
    state_hbm,
    relations_hbm,
    dst_hbm,
    neg_hbm,
    emb_out,
    state_out,
    gathered,
    masks,
    src_ids,
    rel_ids,
    counts,
    emb_in,
    state_in,
    rel_in,
    src_rows,
    rel_rows,
    dst_rows,
    neg_rows,
    emb,
    relations,
    srcs,
    rels,
    table,
    vec,
    far_table,
    far_vec,
    grads,
    is_rel,
    packed,
    x1,
    held_0,
    held_1,
    x2,
    rows_0,
    rows_1,
    vecs_0,
    vecs_1,
    t0,
    r0,
    t1,
    ra,
    t3,
    rz,
    send,
    recv,
    sum_send,
    sum_recv,
    core_send,
    core_recv,
    gather_send,
    gather_recv,
    loaded,
):
    loads = [
        pltpu.make_async_copy(source, target, loaded.at[n])
        for n, (source, target) in enumerate(
            (
                (emb_hbm, emb_in),
                (relations_hbm, rel_in),
                (src_hbm, src_ids),
                (rel_hbm, rel_ids),
                (masks_hbm, masks),
                (counts_hbm, counts),
                (state_hbm, state_in),
                (src_hbm, src_rows),
                (rel_hbm, rel_rows),
                (dst_hbm, dst_rows),
                (neg_hbm, neg_rows),
            )
        )
    ]
    me = lax.axis_index("dom")
    c = me % 2
    y = (me // 2) % 4
    x = (me // 8) % 4
    z = me // 32
    chip = me // 2
    row_mine = (2 * chip + 1) // 5
    vec_mine = ROW_TILES + chip // 5
    has_row = jnp.logical_and(row_carrier(row_mine) == chip, row_mine < ROW_TILES)
    has_vec = jnp.logical_and(vec_carrier(vec_mine) == chip, vec_mine < TILES)
    active = jnp.logical_or(has_row, has_vec)
    idle = jnp.logical_not(active)

    def plane(step):
        return (z + 4 + ((step + 1) // 2) * (1 - 2 * (step % 2))) % 8

    def over_rows(go):
        def first(at):
            return (32 * at + 4) // 5

        def one_plane(step, _):
            at = plane(step)

            def one(i, _):
                go(i, row_carrier(i))
                return 0

            lax.fori_loop(first(at), jnp.minimum(first(at + 1), ROW_TILES), one, 0)
            return 0

        lax.fori_loop(0, 8, one_plane, 0)

    def over_vecs(go):
        def first(at):
            return (16 * at + 3) // 5

        def one_plane(step, _):
            at = plane(step)

            def one(i, _):
                go(ROW_TILES + i, vec_carrier(ROW_TILES + i))
                return 0

            lax.fori_loop(first(at), jnp.minimum(first(at + 1), VEC_TILES), one, 0)
            return 0

        lax.fori_loop(0, 8, one_plane, 0)

    places = [((x + dx) % 4) * 4 + (y + dy) % 4 for dx, dy in OFFSETS]
    place = places[-1]

    def at_place(to):
        return (z * 16 + to) * 2 + c

    def at_z(to):
        return (to * 16 + place) * 2 + c

    other = me + 1 - 2 * c

    barrier = pltpu.get_barrier_semaphore()

    def tell(device):
        pl.semaphore_signal(barrier, inc=1, device_id=(device,), device_id_type=pl.DeviceIdType.MESH)

    def tell_all(step, _):
        def tell_chip(n, _):
            to = 16 * plane(step) + n

            @pl.when(to != chip)
            def _():
                tell(2 * to + c)

            return 0

        lax.fori_loop(0, 16, tell_chip, 0)
        return 0

    def tell_carrier(i, to):
        tell(2 * to + c)

    @pl.when(active)
    def _():
        lax.fori_loop(0, 8, tell_all, 0)

    @pl.when(idle)
    def _():
        over_rows(tell_carrier)
        over_vecs(tell_carrier)

    for to in places[:-1]:
        tell(at_place(to))
    for step in range(7):
        tell(at_z(plane(step)))
    tell(other)
    for load in loads:
        load.start()

    def gather_rels(r):
        for e in range(EDGES):
            rels[r, e : e + 1, :] = relations[pl.ds(rel_ids[r, e], 1), :]

    def gather_srcs(r):
        for e in range(EDGES):
            srcs[r, e : e + 1, :] = emb[pl.ds(src_ids[r, e], 1), :]

    def hit_row(r):
        hits = jnp.sum((iota((ROWS, NEG), 0) == neg_rows[r]).astype(F32), axis=1, keepdims=True)
        return jnp.concatenate([as_row(hits[:128]), as_row(hits[128:])], axis=1)

    def bucket_rows(r):
        dst = dst_rows[r : r + 1, :].astype(F32)
        live = (iota((1, EDGES), 1) < counts[r]).astype(F32)
        return dst, live, hit_row(r)

    def pack(r, first, rows):
        for i in range(8):
            for j in range(3):
                x1[r, first + 3 * i + j] = rows[16 * i : 16 * i + 16, 128 * j : 128 * j + 128]
        last = rows[:, 384:].astype(F32)
        tail = last[:16]
        for g in range(1, 8):
            tail = tail + pltpu.roll(last[16 * g : 16 * g + 16], LEFT * g, 1)
        x1[r, first + 24] = tail.astype(BF16)

    def unpack(arrived, side, first, target, at):
        for i in range(8):
            for j in range(3):
                target[at + 16 * i : at + 16 * i + 16, 128 * j : 128 * j + 128] = arrived[side, first + 3 * i + j]
        tail = arrived[side, first + 24].astype(F32)
        inside = iota((16, 128), 1) < LEFT
        for g in range(8):
            part = pltpu.roll(tail, 128 - LEFT * g, 1) if g else tail
            target[at + 16 * g : at + 16 * g + 16, 384:] = jnp.where(inside, part, 0.0).astype(BF16)

    def pack_table(r):
        table[...] = emb[...].astype(BF16)
        pack(r, 0, table[0:128, :])
        pack(r, 25, table[128:256, :])

    def pack_vectors(r):
        vec[...] = (srcs[r] * rels[r]).astype(BF16)
        pack(r, ROW_TILES, vec[...])

    def pack_meta(r, rows):
        dst, live, hits = rows
        high = jnp.floor(hits * (1.0 / 16.0))
        low = hits - 16.0 * high
        extras = (dst, live, high[:, :128], high[:, 128:], low[:, :128], low[:, 128:])
        sub = iota((16, 128), 0)
        meta = jnp.zeros((16, 128), F32)
        for n, extra in enumerate(extras):
            meta = jnp.where(sub == n, extra, meta)
        x1[r, 50] = meta.astype(BF16)

    def send_out(r, over):
        held = (held_0, held_1)[r]

        def outward(i, to):
            @pl.when(to != chip)
            def _():
                remote(x1.at[r, i], held.at[chip], send.at[r, 0], recv.at[r, 0], 2 * to + c).start()

            @pl.when(to == chip)
            def _():
                held[chip] = x1[r, i]

        over(outward)

    def relay(r, mask, arrived, mine, sem):
        held = (held_0, held_1)[r]
        chip_mask = lax.shift_right_logical(mask, 1)
        await_bytes(held.at[pl.ds(0, CHIPS - 1)], recv.at[r, 0])

        def onward(step, _):
            base = 16 * plane(step)
            for n in range(16):
                x2[r, base + n] = held[lax.bitwise_xor(chip_mask, base + n)]
            for n in places:
                to = base + n

                @pl.when(to != chip)
                def _():
                    remote(x2.at[r, to], arrived.at[0, mine], send.at[r, 1], recv.at[r, sem], 2 * to + c).start()

            return 0

        lax.fori_loop(0, 8, onward, 0)
        arrived[0, mine] = x2[r, chip]

    def take_in(r, has, arrived, count, sem):
        @pl.when(has)
        def _():
            await_bytes(arrived.at[0, pl.ds(0, count - 1)], recv.at[r, sem])

        @pl.when(jnp.logical_not(has))
        def _():
            await_bytes(arrived.at[0], recv.at[r, sem])

        remote(arrived.at[0], arrived.at[1], send.at[r, sem + 1], recv.at[r, sem + 1], other).start()

    def sent(r):
        @pl.when(active)
        def _():
            await_bytes(x1.at[r, pl.ds(0, TILES - 1)], send.at[r, 0])
            await_bytes(x2.at[r, pl.ds(0, CHIPS - 1)], send.at[r, 1])

        @pl.when(idle)
        def _():
            await_bytes(x1.at[r], send.at[r, 0])

        await_bytes(x1.at[r, pl.ds(0, ROW_TILES)], send.at[r, 2])
        await_bytes(x1.at[r, pl.ds(0, VEC_TILES)], send.at[r, 4])

    def coefficients(vectors, rows, ends):
        dst, live, hits = ends
        scores = dot(vectors, rows, 1, 1)
        dst = as_column(dst)
        live = as_column(live)
        is_dst = iota((EDGES, ROWS), 1).astype(F32) == dst
        neg_coef = (live * (1.0 / (1.0 + jnp.exp(-scores))) / NEG).astype(BF16).astype(F32)
        positive = jnp.sum(jnp.where(is_dst, scores, 0.0), axis=1, keepdims=True)
        pos_coef = -live * (1.0 / (1.0 + jnp.exp(positive)))
        return halves(neg_coef * hits + jnp.where(is_dst, pos_coef, 0.0))

    for load in loads:
        load.wait()
    emb[:, 384:] = jnp.zeros((ROWS, 128), F32)
    for j in range(4):
        depth = min(128, D - 128 * j)
        for i in range(2):
            emb[128 * i : 128 * i + 128, 128 * j : 128 * j + depth] = emb_in[
                128 * j : 128 * j + depth, 128 * i : 128 * i + 128
            ].T
    pack_table(0)
    buckets = [bucket_rows(r) for r in range(ROUNDS)]
    for r in range(ROUNDS):
        pack_meta(r, buckets[r])
    state = jnp.concatenate([as_column(state_in[:, :128]), as_column(state_in[:, 128:])], axis=0)

    gather_srcs(0)
    relations[:, 384:] = jnp.zeros((REL_PAD, 128), F32)
    for j in range(4):
        depth = min(128, D - 128 * j)
        for i in range(11):
            width = min(128, NREL - 128 * i)
            part = rel_in[128 * j : 128 * j + depth, 128 * i : 128 * i + width]
            if width < 128:
                part = jnp.concatenate([part, jnp.ones((depth, 128 - width), F32)], axis=1)
            relations[128 * i : 128 * i + 128, 128 * j : 128 * j + depth] = part.T
    for r in range(ROUNDS):
        gather_rels(r)
    pack_vectors(0)

    @pl.when(active)
    def _():
        pl.semaphore_wait(barrier, CHIPS - 1 + 23)

    @pl.when(idle)
    def _():
        pl.semaphore_wait(barrier, TILES + 23)

    def prepare_sum():
        ids = jnp.concatenate([rel_rows[0:1, :], rel_rows[1:2, :]], axis=1)
        for g in range(8):
            at = GROUP * g
            is_rel[at : at + GROUP, :] = (iota((GROUP, ROUNDS * EDGES), 0) + at == ids).astype(BF16)

    for r in range(ROUNDS):
        mask = masks[r]
        side = lax.bitwise_and(mask, 1)
        far_rows = (rows_0, rows_1)[r]
        far_vecs = (vecs_0, vecs_1)[r]
        send_out(r, over_rows)
        if r > 0:
            gather_srcs(r)
            pack_vectors(r)
        if r + 1 < ROUNDS:
            send_out(r, over_vecs)
            prepare_sum()

        @pl.when(has_row)
        def _():
            relay(r, mask, far_rows, row_mine, 1)

        if r + 1 == ROUNDS:
            send_out(r, over_vecs)
        else:

            @pl.when(has_vec)
            def _():
                relay(r, mask, far_vecs, vec_mine - ROW_TILES, 3)

        take_in(r, has_row, far_rows, ROW_TILES, 1)
        await_bytes(far_rows.at[1], recv.at[r, 2])
        unpack(far_rows, side, 0, far_table, 0)
        unpack(far_rows, side, 25, far_table, 128)
        meta = far_rows[side, 50].astype(F32)
        hits = jnp.concatenate([16.0 * meta[n : n + 1] + meta[n + 2 : n + 3] for n in (2, 3)], axis=1)
        far = (meta[0:1], meta[1:2], hits)

        high, low = coefficients(vec[...], far_table[...], buckets[r])
        if r + 1 < ROUNDS:
            take_in(r, has_vec, far_vecs, VEC_TILES, 3)
        pulled = (dot(high, far_table[...]) + dot(low, far_table[...])).astype(BF16).astype(F32)
        grads[r * EDGES : (r + 1) * EDGES, :] = (pulled * srcs[r]).astype(BF16)

        def update_rows(r, state, pulled, far, far_vecs, side):
            is_src = (iota((ROWS, EDGES), 0) == src_rows[r : r + 1, :]).astype(BF16)
            high, low = halves(pulled * rels[r])
            grad = dot(is_src, high) + dot(is_src, low)
            if r + 1 == ROUNDS:
                take_in(r, has_vec, far_vecs, VEC_TILES, 3)
            await_bytes(far_vecs.at[1], recv.at[r, 4])
            unpack(far_vecs, side, 0, far_vec, 0)
            high, low = coefficients(far_vec[...], table[...], far)
            pushed = dot(high, far_vec[...], 0, 0) + dot(low, far_vec[...], 0, 0)
            grad = grad + pushed.astype(BF16).astype(F32)
            state = state + jnp.sum(grad * grad, axis=1, keepdims=True) * (1.0 / D)
            emb[...] = emb[...] - grad * (learning_rate / jnp.sqrt(state))
            return state

        if r + 1 < ROUNDS:
            state = update_rows(r, state, pulled, far, far_vecs, side)
            pack_table(r + 1)

    tail = jnp.zeros((GROUP, 128), F32)
    for g in range(8):
        rows = min(GROUP, BLOCK - GROUP * g)
        part = dot(is_rel[GROUP * g : GROUP * g + GROUP, :], grads[...])
        for n in range(3):
            at = BLOCK * n + GROUP * g
            packed[at : at + rows, :] = part[:rows, 128 * n : 128 * n + 128]
        end = part[:, 384:]
        tail = tail + (pltpu.roll(end, LEFT * g, 1) if g else end)
    packed[3 * BLOCK : 3 * BLOCK + GROUP, :] = tail
    packed[3 * BLOCK + GROUP :, :] = jnp.zeros((PACKED - 3 * BLOCK - GROUP, 128), F32)

    def partial(half, to):
        rows = pl.ds(pl.multiple_of(2048 * half + 128 * to, 128), 128)
        return packed[rows, :].reshape(8, 16, 128)

    for k, to in enumerate(places):
        piece = pl.ds(8 * to, 8)
        t0[piece] = partial(1 - c, to).astype(BF16)
        remote(t0.at[piece], r0.at[piece], core_send.at[k], core_recv.at[k], other).start()
    for k, to in enumerate(places):
        piece = pl.ds(8 * to, 8)
        await_bytes(r0.at[piece], core_recv.at[k])
        t1[piece] = (partial(c, to) + r0[piece].astype(F32)).astype(BF16)
        if k < 15:
            remote(t1.at[piece], ra.at[place], sum_send.at[0], sum_recv.at[0], at_place(to)).start()
    ra[place] = t1[pl.ds(8 * place, 8)]

    @pl.when(has_vec)
    def _():
        relay(r, mask, far_vecs, vec_mine - ROW_TILES, 3)

    await_bytes(ra.at[pl.ds(0, 15)], sum_recv.at[0])

    def added(ref, count):
        total = ref[0].astype(F32)
        for n in range(1, count):
            total = total + ref[n].astype(F32)
        return total.astype(BF16)

    t3[...] = added(ra, 16)
    for step in range(7):
        to = plane(step)
        remote(t3.at[to], rz.at[z], sum_send.at[1], sum_recv.at[1], at_z(to)).start()
    rz[z] = t3[z]
    await_bytes(rz.at[pl.ds(0, 7)], sum_recv.at[1])

    base = c * 128 + 8 * place
    spot = base + z
    gathered[spot] = added(rz, 8)
    for step in range(7):
        to = plane(step)
        remote(gathered.at[spot], gathered.at[spot], sum_send.at[2], sum_recv.at[2], at_z(to)).start()
    await_bytes(gathered.at[pl.ds(0, 7)], sum_recv.at[2])

    own = gathered.at[pl.ds(base, 8)]
    for k, to in enumerate(places[:-1]):
        dx, dy = OFFSETS[k]
        back = OFFSETS.index((-dx % 4, -dy % 4))
        remote(own, own, gather_send.at[k], gather_recv.at[back], at_place(to)).start()
    state = update_rows(r, state, pulled, far, far_vecs, side)
    for k, to in [(15, place)] + list(enumerate(places[:-1])):
        piece = gathered.at[pl.ds(c * 128 + 8 * to, 8)]
        if k < 15:
            await_bytes(piece, gather_recv.at[k])
        remote(piece, piece, sum_send.at[3], sum_recv.at[3], other).start()
    for j in range(4):
        depth = min(128, D - 128 * j)
        for i in range(2):
            part = emb[128 * i : 128 * i + 128, 128 * j : 128 * j + 128].T
            emb_out[128 * j : 128 * j + depth, 128 * i : 128 * i + 128] = part[:depth]
    state_out[...] = jnp.concatenate([as_row(state[:128]), as_row(state[128:])], axis=1)
    await_bytes(gathered.at[pl.ds(0, 128)], sum_recv.at[3])

    for r in range(ROUNDS):
        sent(r)
    for k in range(16):
        await_bytes(r0.at[pl.ds(0, 8)], core_send.at[k])
    for n, tiles in ((0, 120), (1, 7), (2, 7), (3, 128)):
        await_bytes(gathered.at[pl.ds(0, tiles)], sum_send.at[n])
    for k in range(15):
        await_bytes(gathered.at[pl.ds(0, 8)], gather_send.at[k])


def finish(
    emb_hbm,
    state_hbm,
    sums_hbm,
    rel_hbm,
    rel_state_hbm,
    emb_out,
    state_out,
    rel_out,
    rel_state_out,
    sums,
    rel_in,
    state_in,
    rel_state_in,
    packed,
    tails,
    rel_new,
    state_new,
    rel_state_new,
    emb_kept,
    sems,
):
    loads = [
        pltpu.make_async_copy(sums_hbm, sums, sems.at[0]),
        pltpu.make_async_copy(rel_state_hbm, rel_state_in, sems.at[1]),
        pltpu.make_async_copy(rel_hbm, rel_in, sems.at[2]),
        pltpu.make_async_copy(state_hbm, state_in, sems.at[3]),
    ]
    loads.append(pltpu.make_async_copy(emb_hbm, emb_kept, sems.at[4]))
    for load in loads:
        load.start()
    for load in loads:
        load.wait()
    state_new[...] = state_in[...].reshape(ROWS)
    stores = [
        pltpu.make_async_copy(state_new, state_out, sems.at[5]),
        pltpu.make_async_copy(emb_kept, emb_out, sems.at[8]),
    ]
    for store in stores:
        store.start()
    packed[...] = sums[...].astype(F32).reshape(PACKED, 128)
    end = packed[3 * BLOCK : 3 * BLOCK + GROUP, :]
    inside = iota((GROUP, 128), 1) < LEFT
    for g in range(8):
        part = pltpu.roll(end, 128 - LEFT * g, 1) if g else end
        tails[GROUP * g : GROUP * g + GROUP, :] = jnp.where(inside, part, 0.0)
    tails[8 * GROUP :, :] = jnp.zeros((REL_PAD - 8 * GROUP, 128), F32)
    for i in range(11):
        at = 128 * i
        width = min(128, NREL - at)
        rows = min(128, BLOCK - at)
        parts = [packed[BLOCK * n + at : BLOCK * n + at + rows, :] for n in range(3)] + [tails[at : at + rows, :]]
        if rows < 128:
            parts = [jnp.concatenate([part, jnp.zeros((128 - rows, 128), F32)], axis=0) for part in parts]
        old = rel_state_in[at : at + width].reshape(1, width)
        if width < 128:
            old = jnp.concatenate([old, jnp.ones((1, 128 - width), F32)], axis=1)
        squares = parts[0] * parts[0] + parts[1] * parts[1] + parts[2] * parts[2] + parts[3] * parts[3]
        fresh = old + as_row(jnp.sum(squares, axis=1, keepdims=True)) * (1.0 / D)
        rel_state_new[at : at + width] = fresh[:, :width].reshape(width)
        scale = learning_rate / jnp.sqrt(fresh)
        for n in range(4):
            depth = min(128, D - 128 * n)
            change = parts[n].T[:depth] * scale
            cols = slice(128 * n, 128 * n + depth)
            rel_new[cols, at : at + width] = rel_in[cols, at : at + width] - change[:, :width]
    stores.append(pltpu.make_async_copy(rel_new, rel_out, sems.at[6]))
    stores.append(pltpu.make_async_copy(rel_state_new, rel_state_out, sems.at[7]))
    for store in stores[2:]:
        store.start()
    for store in stores:
        store.wait()


def shards(
    embeddings,
    entity_state,
    relations,
    relation_state,
    round_masks,
    edge_src,
    edge_rel,
    edge_dst,
    edge_count,
    neg_rows,
):
    vmem = pl.BlockSpec(memory_space=pltpu.VMEM)

    def tiles(*lead):
        return pltpu.VMEM(lead + (16, 128), BF16)

    hbm = pl.BlockSpec(memory_space=pltpu.HBM)
    rows_t, state, sums = pl.pallas_call(
        kernel,
        out_shape=(
            jax.ShapeDtypeStruct((D, ROWS), F32),
            jax.ShapeDtypeStruct((1, ROWS), F32),
            jax.ShapeDtypeStruct((256, 16, 128), BF16),
        ),
        in_specs=[hbm] * 9,
        out_specs=(vmem,) * 3,
        scratch_shapes=[
            pltpu.SMEM((ROUNDS,), jnp.int32),
            pltpu.SMEM((ROUNDS, EDGES), jnp.int32),
            pltpu.SMEM((ROUNDS, EDGES), jnp.int32),
            pltpu.SMEM((ROUNDS,), jnp.int32),
            pltpu.VMEM((D, ROWS), F32),
            pltpu.VMEM((1, ROWS), F32),
            pltpu.VMEM((D, NREL), F32),
            pltpu.VMEM((ROUNDS, EDGES), jnp.int32),
            pltpu.VMEM((ROUNDS, EDGES), jnp.int32),
            pltpu.VMEM((ROUNDS, EDGES), jnp.int32),
            pltpu.VMEM((ROUNDS, 1, NEG), jnp.int32),
            pltpu.VMEM((ROWS, WIDE), F32),
            pltpu.VMEM((REL_PAD, WIDE), F32),
            pltpu.VMEM((ROUNDS, EDGES, WIDE), F32),
            pltpu.VMEM((ROUNDS, EDGES, WIDE), F32),
            pltpu.VMEM((ROWS, WIDE), BF16),
            pltpu.VMEM((EDGES, WIDE), BF16),
            pltpu.VMEM((ROWS, WIDE), BF16),
            pltpu.VMEM((EDGES, WIDE), BF16),
            pltpu.VMEM((ROUNDS * EDGES, WIDE), BF16),
            pltpu.VMEM((8 * GROUP, ROUNDS * EDGES), BF16),
            pltpu.VMEM((PACKED, 128), F32),
            tiles(ROUNDS, TILES),
            tiles(CHIPS),
            tiles(CHIPS),
            tiles(ROUNDS, CHIPS),
            tiles(2, ROW_TILES),
            tiles(2, ROW_TILES),
            tiles(2, VEC_TILES),
            tiles(2, VEC_TILES),
            tiles(128),
            tiles(128),
            tiles(128),
            tiles(16, 8),
            tiles(8),
            tiles(8),
            pltpu.SemaphoreType.DMA((ROUNDS, 5)),
            pltpu.SemaphoreType.DMA((ROUNDS, 5)),
            pltpu.SemaphoreType.DMA((4,)),
            pltpu.SemaphoreType.DMA((4,)),
            pltpu.SemaphoreType.DMA((16,)),
            pltpu.SemaphoreType.DMA((16,)),
            pltpu.SemaphoreType.DMA((15,)),
            pltpu.SemaphoreType.DMA((15,)),
            pltpu.SemaphoreType.DMA((12,)),
        ],
        compiler_params=pltpu.CompilerParams(
            collective_id=0, has_side_effects=True, vmem_limit_bytes=60 * 1024 * 1024
        ),
    )(
        round_masks,
        edge_src,
        edge_rel,
        edge_count.reshape(ROUNDS),
        embeddings.T,
        entity_state.reshape(1, ROWS),
        relations.T,
        edge_dst,
        neg_rows,
    )
    new_rows, new_state, new_relations, new_relation_state = pl.pallas_call(
        finish,
        out_shape=(
            jax.ShapeDtypeStruct((D, ROWS), F32),
            jax.ShapeDtypeStruct((ROWS,), F32),
            jax.ShapeDtypeStruct((D, NREL), F32),
            jax.ShapeDtypeStruct((NREL,), F32),
        ),
        in_specs=[hbm] * 5,
        out_specs=(hbm,) * 4,
        scratch_shapes=[
            tiles(256),
            pltpu.VMEM((D, NREL), F32),
            pltpu.VMEM((1, ROWS), F32),
            pltpu.VMEM((NREL,), F32),
            pltpu.VMEM((PACKED, 128), F32),
            pltpu.VMEM((REL_PAD, 128), F32),
            pltpu.VMEM((D, NREL), F32),
            pltpu.VMEM((ROWS,), F32),
            pltpu.VMEM((NREL,), F32),
            pltpu.VMEM((D, ROWS), F32),
            pltpu.SemaphoreType.DMA((9,)),
        ],
        compiler_params=pltpu.CompilerParams(vmem_limit_bytes=60 * 1024 * 1024),
    )(rows_t, state, sums, relations.T, relation_state)
    return (new_rows.T, new_state, new_relations.T, new_relation_state)


def solution(mesh):
    placed = (
        P("dom", None),
        P("dom"),
        P(),
        P(),
        P(),
        P(None, "dom"),
        P(None, "dom"),
        P(None, "dom"),
        P(None, "dom"),
        P(None, "dom", None),
    )
    return jax.shard_map(
        shards,
        mesh=mesh,
        in_specs=placed,
        out_specs=(P("dom", None), P("dom"), P(), P()),
        check_vma=False,
    )
```

```python
import jax
import jax.numpy as jnp
from jax import lax
from jax.experimental import pallas as pl
from jax.experimental.pallas import tpu as pltpu
from jax.sharding import PartitionSpec as P

ROUNDS = 2
D = 400
NREL = 1300
NEG = 1000
ROWS = 256
EDGES = 128
WIDE = 512
LEFT = D - 384
CHIPS = 128
TILES = 76
ROW_TILES = 51
VEC_TILES = 25
REL_PAD = 1408
BLOCK = 1304
GROUP = 168
PACKED = 4096

learning_rate = 0.1

F32 = jnp.float32
BF16 = jnp.bfloat16


def iota(shape, dim):
    return lax.broadcasted_iota(jnp.int32, shape, dim)


def dot(a, b, left=1, right=0):
    return lax.dot_general(a, b, (((left,), (right,)), ((), ())), preferred_element_type=F32)


def halves(value):
    high = value.astype(BF16)
    return high, (value - high.astype(F32)).astype(BF16)


def as_column(row):
    count = row.shape[1]
    square = (count, count)
    return jnp.sum(jnp.where(iota(square, 0) == iota(square, 1), row, 0.0), axis=1, keepdims=True)


def as_row(column):
    count = column.shape[0]
    square = (count, count)
    return jnp.sum(jnp.where(iota(square, 0) == iota(square, 1), column, 0.0), axis=0, keepdims=True)


def remote(source, target, send, recv, device):
    return pltpu.make_async_remote_copy(
        src_ref=source,
        dst_ref=target,
        send_sem=send,
        recv_sem=recv,
        device_id=(device,),
        device_id_type=pl.DeviceIdType.MESH,
    )


def await_bytes(ref, sem):
    pltpu.make_async_copy(ref, ref, sem).wait()


def ring(offset):
    return min(offset, 4 - offset)


OFFSETS = sorted(
    ((dx, dy) for dx in range(4) for dy in range(4)),
    key=lambda offset: -ring(offset[0]) - ring(offset[1]),
)


def row_carrier(tile):
    return (5 * tile) // 2


def vec_carrier(tile):
    return 5 * (tile - ROW_TILES) + 1


def kernel(
    masks_hbm,
    src_hbm,
    rel_hbm,
    counts_hbm,
    emb_hbm,
    state_hbm,
    relations_hbm,
    dst_hbm,
    neg_hbm,
    emb_out,
    state_out,
    gathered,
    masks,
    src_ids,
    rel_ids,
    counts,
    emb_in,
    state_in,
    rel_in,
    src_rows,
    rel_rows,
    dst_rows,
    neg_rows,
    emb,
    relations,
    srcs,
    rels,
    table,
    vec,
    far_table,
    far_vec,
    grads,
    is_rel,
    packed,
    x1,
    held_0,
    held_1,
    x2,
    rows_0,
    rows_1,
    vecs_0,
    vecs_1,
    t0,
    r0,
    t1,
    ra,
    t3,
    rz,
    send,
    recv,
    sum_send,
    sum_recv,
    core_send,
    core_recv,
    gather_send,
    gather_recv,
    loaded,
):
    loads = [
        pltpu.make_async_copy(source, target, loaded.at[n])
        for n, (source, target) in enumerate(
            (
                (emb_hbm, emb_in),
                (relations_hbm, rel_in),
                (src_hbm, src_ids),
                (rel_hbm, rel_ids),
                (masks_hbm, masks),
                (counts_hbm, counts),
                (state_hbm, state_in),
                (src_hbm, src_rows),
                (rel_hbm, rel_rows),
                (dst_hbm, dst_rows),
                (neg_hbm, neg_rows),
            )
        )
    ]
    me = lax.axis_index("dom")
    c = me % 2
    y = (me // 2) % 4
    x = (me // 8) % 4
    z = me // 32
    chip = me // 2
    row_mine = (2 * chip + 1) // 5
    vec_mine = ROW_TILES + chip // 5
    has_row = jnp.logical_and(row_carrier(row_mine) == chip, row_mine < ROW_TILES)
    has_vec = jnp.logical_and(vec_carrier(vec_mine) == chip, vec_mine < TILES)
    active = jnp.logical_or(has_row, has_vec)
    idle = jnp.logical_not(active)

    def plane(step):
        return (z + 4 + ((step + 1) // 2) * (1 - 2 * (step % 2))) % 8

    def over_rows(go):
        def first(at):
            return (32 * at + 4) // 5

        def one_plane(step, _):
            at = plane(step)

            def one(i, _):
                go(i, row_carrier(i))
                return 0

            lax.fori_loop(first(at), jnp.minimum(first(at + 1), ROW_TILES), one, 0)
            return 0

        lax.fori_loop(0, 8, one_plane, 0)

    def over_vecs(go):
        def first(at):
            return (16 * at + 3) // 5

        def one_plane(step, _):
            at = plane(step)

            def one(i, _):
                go(ROW_TILES + i, vec_carrier(ROW_TILES + i))
                return 0

            lax.fori_loop(first(at), jnp.minimum(first(at + 1), VEC_TILES), one, 0)
            return 0

        lax.fori_loop(0, 8, one_plane, 0)

    places = [((x + dx) % 4) * 4 + (y + dy) % 4 for dx, dy in OFFSETS]
    place = places[-1]

    def at_place(to):
        return (z * 16 + to) * 2 + c

    def at_z(to):
        return (to * 16 + place) * 2 + c

    other = me + 1 - 2 * c

    barrier = pltpu.get_barrier_semaphore()

    def tell(device):
        pl.semaphore_signal(barrier, inc=1, device_id=(device,), device_id_type=pl.DeviceIdType.MESH)

    def tell_all(step, _):
        def tell_chip(n, _):
            to = 16 * plane(step) + n

            @pl.when(to != chip)
            def _():
                tell(2 * to + c)

            return 0

        lax.fori_loop(0, 16, tell_chip, 0)
        return 0

    def tell_carrier(i, to):
        tell(2 * to + c)

    @pl.when(active)
    def _():
        lax.fori_loop(0, 8, tell_all, 0)

    @pl.when(idle)
    def _():
        over_rows(tell_carrier)
        over_vecs(tell_carrier)

    for to in places[:-1]:
        tell(at_place(to))
    for step in range(7):
        tell(at_z(plane(step)))
    tell(other)
    for load in loads:
        load.start()

    def gather_rels(r):
        for e in range(EDGES):
            rels[r, e : e + 1, :] = relations[pl.ds(rel_ids[r, e], 1), :]

    def gather_srcs(r):
        for e in range(EDGES):
            srcs[r, e : e + 1, :] = emb[pl.ds(src_ids[r, e], 1), :]

    def hit_row(r):
        hits = jnp.sum((iota((ROWS, NEG), 0) == neg_rows[r]).astype(F32), axis=1, keepdims=True)
        return jnp.concatenate([as_row(hits[:128]), as_row(hits[128:])], axis=1)

    def bucket_rows(r):
        dst = dst_rows[r : r + 1, :].astype(F32)
        live = (iota((1, EDGES), 1) < counts[r]).astype(F32)
        return dst, live, hit_row(r)

    def pack(r, first, rows):
        for i in range(8):
            for j in range(3):
                x1[r, first + 3 * i + j] = rows[16 * i : 16 * i + 16, 128 * j : 128 * j + 128]
        last = rows[:, 384:].astype(F32)
        tail = last[:16]
        for g in range(1, 8):
            tail = tail + pltpu.roll(last[16 * g : 16 * g + 16], LEFT * g, 1)
        x1[r, first + 24] = tail.astype(BF16)

    def unpack(arrived, side, first, target, at):
        for i in range(8):
            for j in range(3):
                target[at + 16 * i : at + 16 * i + 16, 128 * j : 128 * j + 128] = arrived[side, first + 3 * i + j]
        tail = arrived[side, first + 24].astype(F32)
        inside = iota((16, 128), 1) < LEFT
        for g in range(8):
            part = pltpu.roll(tail, 128 - LEFT * g, 1) if g else tail
            target[at + 16 * g : at + 16 * g + 16, 384:] = jnp.where(inside, part, 0.0).astype(BF16)

    def pack_table(r):
        table[...] = emb[...].astype(BF16)
        pack(r, 0, table[0:128, :])
        pack(r, 25, table[128:256, :])

    def pack_vectors(r):
        vec[...] = (srcs[r] * rels[r]).astype(BF16)
        pack(r, ROW_TILES, vec[...])

    def pack_meta(r, rows):
        dst, live, hits = rows
        high = jnp.floor(hits * (1.0 / 16.0))
        low = hits - 16.0 * high
        extras = (dst, live, high[:, :128], high[:, 128:], low[:, :128], low[:, 128:])
        sub = iota((16, 128), 0)
        meta = jnp.zeros((16, 128), F32)
        for n, extra in enumerate(extras):
            meta = jnp.where(sub == n, extra, meta)
        x1[r, 50] = meta.astype(BF16)

    def send_out(r, over):
        held = (held_0, held_1)[r]

        def outward(i, to):
            @pl.when(to != chip)
            def _():
                remote(x1.at[r, i], held.at[chip], send.at[r, 0], recv.at[r, 0], 2 * to + c).start()

            @pl.when(to == chip)
            def _():
                held[chip] = x1[r, i]

        over(outward)

    def relay(r, mask, arrived, mine, sem):
        held = (held_0, held_1)[r]
        chip_mask = lax.shift_right_logical(mask, 1)
        await_bytes(held.at[pl.ds(0, CHIPS - 1)], recv.at[r, 0])

        def onward(step, _):
            base = 16 * plane(step)
            for n in range(16):
                x2[r, base + n] = held[lax.bitwise_xor(chip_mask, base + n)]
            for n in places:
                to = base + n

                @pl.when(to != chip)
                def _():
                    remote(x2.at[r, to], arrived.at[0, mine], send.at[r, 1], recv.at[r, sem], 2 * to + c).start()

            return 0

        lax.fori_loop(0, 8, onward, 0)
        arrived[0, mine] = x2[r, chip]

    def take_in(r, has, arrived, count, sem):
        @pl.when(has)
        def _():
            await_bytes(arrived.at[0, pl.ds(0, count - 1)], recv.at[r, sem])

        @pl.when(jnp.logical_not(has))
        def _():
            await_bytes(arrived.at[0], recv.at[r, sem])

        remote(arrived.at[0], arrived.at[1], send.at[r, sem + 1], recv.at[r, sem + 1], other).start()

    def sent(r):
        @pl.when(active)
        def _():
            await_bytes(x1.at[r, pl.ds(0, TILES - 1)], send.at[r, 0])
            await_bytes(x2.at[r, pl.ds(0, CHIPS - 1)], send.at[r, 1])

        @pl.when(idle)
        def _():
            await_bytes(x1.at[r], send.at[r, 0])

        await_bytes(x1.at[r, pl.ds(0, ROW_TILES)], send.at[r, 2])
        await_bytes(x1.at[r, pl.ds(0, VEC_TILES)], send.at[r, 4])

    def coefficients(vectors, rows, ends):
        dst, live, hits = ends
        scores = dot(vectors, rows, 1, 1)
        dst = as_column(dst)
        live = as_column(live)
        is_dst = iota((EDGES, ROWS), 1).astype(F32) == dst
        neg_coef = (live * (1.0 / (1.0 + jnp.exp(-scores))) / NEG).astype(BF16).astype(F32)
        positive = jnp.sum(jnp.where(is_dst, scores, 0.0), axis=1, keepdims=True)
        pos_coef = -live * (1.0 / (1.0 + jnp.exp(positive)))
        return halves(neg_coef * hits + jnp.where(is_dst, pos_coef, 0.0))

    for load in loads:
        load.wait()
    emb[:, 384:] = jnp.zeros((ROWS, 128), F32)
    for j in range(4):
        depth = min(128, D - 128 * j)
        for i in range(2):
            emb[128 * i : 128 * i + 128, 128 * j : 128 * j + depth] = emb_in[
                128 * j : 128 * j + depth, 128 * i : 128 * i + 128
            ].T
    pack_table(0)
    buckets = [bucket_rows(r) for r in range(ROUNDS)]
    for r in range(ROUNDS):
        pack_meta(r, buckets[r])
    state = jnp.concatenate([as_column(state_in[:, :128]), as_column(state_in[:, 128:])], axis=0)

    gather_srcs(0)
    relations[:, 384:] = jnp.zeros((REL_PAD, 128), F32)
    for j in range(4):
        depth = min(128, D - 128 * j)
        for i in range(11):
            width = min(128, NREL - 128 * i)
            part = rel_in[128 * j : 128 * j + depth, 128 * i : 128 * i + width]
            if width < 128:
                part = jnp.concatenate([part, jnp.ones((depth, 128 - width), F32)], axis=1)
            relations[128 * i : 128 * i + 128, 128 * j : 128 * j + depth] = part.T
    for r in range(ROUNDS):
        gather_rels(r)
    pack_vectors(0)

    @pl.when(active)
    def _():
        pl.semaphore_wait(barrier, CHIPS - 1 + 23)

    @pl.when(idle)
    def _():
        pl.semaphore_wait(barrier, TILES + 23)

    def prepare_sum():
        ids = jnp.concatenate([rel_rows[0:1, :], rel_rows[1:2, :]], axis=1)
        for g in range(8):
            at = GROUP * g
            is_rel[at : at + GROUP, :] = (iota((GROUP, ROUNDS * EDGES), 0) + at == ids).astype(BF16)

    for r in range(ROUNDS):
        mask = masks[r]
        side = lax.bitwise_and(mask, 1)
        far_rows = (rows_0, rows_1)[r]
        far_vecs = (vecs_0, vecs_1)[r]
        send_out(r, over_rows)
        if r > 0:
            gather_srcs(r)
            pack_vectors(r)
        if r + 1 < ROUNDS:
            send_out(r, over_vecs)
            prepare_sum()

        @pl.when(has_row)
        def _():
            relay(r, mask, far_rows, row_mine, 1)

        if r + 1 == ROUNDS:
            send_out(r, over_vecs)
        else:

            @pl.when(has_vec)
            def _():
                relay(r, mask, far_vecs, vec_mine - ROW_TILES, 3)

        take_in(r, has_row, far_rows, ROW_TILES, 1)
        await_bytes(far_rows.at[1], recv.at[r, 2])
        unpack(far_rows, side, 0, far_table, 0)
        unpack(far_rows, side, 25, far_table, 128)
        meta = far_rows[side, 50].astype(F32)
        hits = jnp.concatenate([16.0 * meta[n : n + 1] + meta[n + 2 : n + 3] for n in (2, 3)], axis=1)
        far = (meta[0:1], meta[1:2], hits)

        high, low = coefficients(vec[...], far_table[...], buckets[r])
        if r + 1 < ROUNDS:
            take_in(r, has_vec, far_vecs, VEC_TILES, 3)
        pulled = (dot(high, far_table[...]) + dot(low, far_table[...])).astype(BF16).astype(F32)
        grads[r * EDGES : (r + 1) * EDGES, :] = (pulled * srcs[r]).astype(BF16)

        def update_rows(r, state, pulled, far, far_vecs, side):
            is_src = (iota((ROWS, EDGES), 0) == src_rows[r : r + 1, :]).astype(BF16)
            high, low = halves(pulled * rels[r])
            grad = dot(is_src, high) + dot(is_src, low)
            if r + 1 == ROUNDS:
                take_in(r, has_vec, far_vecs, VEC_TILES, 3)
            await_bytes(far_vecs.at[1], recv.at[r, 4])
            unpack(far_vecs, side, 0, far_vec, 0)
            high, low = coefficients(far_vec[...], table[...], far)
            pushed = dot(high, far_vec[...], 0, 0) + dot(low, far_vec[...], 0, 0)
            grad = grad + pushed.astype(BF16).astype(F32)
            state = state + jnp.sum(grad * grad, axis=1, keepdims=True) * (1.0 / D)
            emb[...] = emb[...] - grad * (learning_rate / jnp.sqrt(state))
            return state

        if r + 1 < ROUNDS:
            state = update_rows(r, state, pulled, far, far_vecs, side)
            pack_table(r + 1)

    tail = jnp.zeros((GROUP, 128), F32)
    for g in range(8):
        rows = min(GROUP, BLOCK - GROUP * g)
        part = dot(is_rel[GROUP * g : GROUP * g + GROUP, :], grads[...])
        for n in range(3):
            at = BLOCK * n + GROUP * g
            packed[at : at + rows, :] = part[:rows, 128 * n : 128 * n + 128]
        end = part[:, 384:]
        tail = tail + (pltpu.roll(end, LEFT * g, 1) if g else end)
    packed[3 * BLOCK : 3 * BLOCK + GROUP, :] = tail
    packed[3 * BLOCK + GROUP :, :] = jnp.zeros((PACKED - 3 * BLOCK - GROUP, 128), F32)

    def partial(half, to):
        rows = pl.ds(pl.multiple_of(2048 * half + 128 * to, 128), 128)
        return packed[rows, :].reshape(8, 16, 128)

    for k, to in enumerate(places):
        piece = pl.ds(8 * to, 8)
        t0[piece] = partial(1 - c, to).astype(BF16)
        remote(t0.at[piece], r0.at[piece], core_send.at[k], core_recv.at[k], other).start()
    for k, to in enumerate(places):
        piece = pl.ds(8 * to, 8)
        await_bytes(r0.at[piece], core_recv.at[k])
        t1[piece] = (partial(c, to) + r0[piece].astype(F32)).astype(BF16)
        if k < 15:
            remote(t1.at[piece], ra.at[place], sum_send.at[0], sum_recv.at[0], at_place(to)).start()
    ra[place] = t1[pl.ds(8 * place, 8)]

    @pl.when(has_vec)
    def _():
        relay(r, mask, far_vecs, vec_mine - ROW_TILES, 3)

    await_bytes(ra.at[pl.ds(0, 15)], sum_recv.at[0])

    def added(ref, count):
        total = ref[0].astype(F32)
        for n in range(1, count):
            total = total + ref[n].astype(F32)
        return total.astype(BF16)

    t3[...] = added(ra, 16)
    for step in range(7):
        remote(t3, rz.at[z], sum_send.at[1], sum_recv.at[1], at_z(plane(step))).start()
    rz[z] = t3[...]
    await_bytes(rz.at[pl.ds(0, 7)], sum_recv.at[1])

    base = c * 128 + 8 * place
    gathered[pl.ds(base, 8)] = added(rz, 8)
    own = gathered.at[pl.ds(base, 8)]
    for k, to in enumerate(places[:-1]):
        dx, dy = OFFSETS[k]
        back = OFFSETS.index((-dx % 4, -dy % 4))
        remote(own, own, gather_send.at[k], gather_recv.at[back], at_place(to)).start()
    state = update_rows(r, state, pulled, far, far_vecs, side)
    for k, to in [(15, place)] + list(enumerate(places[:-1])):
        piece = gathered.at[pl.ds(c * 128 + 8 * to, 8)]
        if k < 15:
            await_bytes(piece, gather_recv.at[k])
        remote(piece, piece, sum_send.at[3], sum_recv.at[3], other).start()
    for j in range(4):
        depth = min(128, D - 128 * j)
        for i in range(2):
            part = emb[128 * i : 128 * i + 128, 128 * j : 128 * j + 128].T
            emb_out[128 * j : 128 * j + depth, 128 * i : 128 * i + 128] = part[:depth]
    state_out[...] = jnp.concatenate([as_row(state[:128]), as_row(state[128:])], axis=1)
    await_bytes(gathered.at[pl.ds(0, 128)], sum_recv.at[3])

    for r in range(ROUNDS):
        sent(r)
    for k in range(16):
        await_bytes(r0.at[pl.ds(0, 8)], core_send.at[k])
    for n, tiles in ((0, 120), (1, 56), (3, 128)):
        await_bytes(gathered.at[pl.ds(0, tiles)], sum_send.at[n])
    for k in range(15):
        await_bytes(gathered.at[pl.ds(0, 8)], gather_send.at[k])


def finish(
    emb_hbm,
    state_hbm,
    sums_hbm,
    rel_hbm,
    rel_state_hbm,
    emb_out,
    state_out,
    rel_out,
    rel_state_out,
    sums,
    rel_in,
    state_in,
    rel_state_in,
    packed,
    tails,
    rel_new,
    state_new,
    rel_state_new,
    emb_kept,
    sems,
):
    loads = [
        pltpu.make_async_copy(sums_hbm, sums, sems.at[0]),
        pltpu.make_async_copy(rel_state_hbm, rel_state_in, sems.at[1]),
        pltpu.make_async_copy(rel_hbm, rel_in, sems.at[2]),
        pltpu.make_async_copy(state_hbm, state_in, sems.at[3]),
    ]
    loads.append(pltpu.make_async_copy(emb_hbm, emb_kept, sems.at[4]))
    for load in loads:
        load.start()
    for load in loads[:2]:
        load.wait()
    packed[...] = sums[...].astype(F32).reshape(PACKED, 128)
    for load in loads[2:]:
        load.wait()
    state_new[...] = state_in[...].reshape(ROWS)
    stores = [
        pltpu.make_async_copy(state_new, state_out, sems.at[5]),
        pltpu.make_async_copy(emb_kept, emb_out, sems.at[8]),
    ]
    for store in stores:
        store.start()
    end = packed[3 * BLOCK : 3 * BLOCK + GROUP, :]
    inside = iota((GROUP, 128), 1) < LEFT
    for g in range(8):
        part = pltpu.roll(end, 128 - LEFT * g, 1) if g else end
        tails[GROUP * g : GROUP * g + GROUP, :] = jnp.where(inside, part, 0.0)
    tails[8 * GROUP :, :] = jnp.zeros((REL_PAD - 8 * GROUP, 128), F32)
    for i in range(11):
        at = 128 * i
        width = min(128, NREL - at)
        rows = min(128, BLOCK - at)
        parts = [packed[BLOCK * n + at : BLOCK * n + at + rows, :] for n in range(3)] + [tails[at : at + rows, :]]
        if rows < 128:
            parts = [jnp.concatenate([part, jnp.zeros((128 - rows, 128), F32)], axis=0) for part in parts]
        old = rel_state_in[at : at + width].reshape(1, width)
        if width < 128:
            old = jnp.concatenate([old, jnp.ones((1, 128 - width), F32)], axis=1)
        squares = parts[0] * parts[0] + parts[1] * parts[1] + parts[2] * parts[2] + parts[3] * parts[3]
        fresh = old + as_row(jnp.sum(squares, axis=1, keepdims=True)) * (1.0 / D)
        rel_state_new[at : at + width] = fresh[:, :width].reshape(width)
        scale = learning_rate / jnp.sqrt(fresh)
        for n in range(4):
            depth = min(128, D - 128 * n)
            change = parts[n].T[:depth] * scale
            cols = slice(128 * n, 128 * n + depth)
            rel_new[cols, at : at + width] = rel_in[cols, at : at + width] - change[:, :width]
    stores.append(pltpu.make_async_copy(rel_new, rel_out, sems.at[6]))
    stores.append(pltpu.make_async_copy(rel_state_new, rel_state_out, sems.at[7]))
    for store in stores[2:]:
        store.start()
    for store in stores:
        store.wait()


def shards(
    embeddings,
    entity_state,
    relations,
    relation_state,
    round_masks,
    edge_src,
    edge_rel,
    edge_dst,
    edge_count,
    neg_rows,
):
    vmem = pl.BlockSpec(memory_space=pltpu.VMEM)

    def tiles(*lead):
        return pltpu.VMEM(lead + (16, 128), BF16)

    hbm = pl.BlockSpec(memory_space=pltpu.HBM)
    rows_t, state, sums = pl.pallas_call(
        kernel,
        out_shape=(
            jax.ShapeDtypeStruct((D, ROWS), F32),
            jax.ShapeDtypeStruct((1, ROWS), F32),
            jax.ShapeDtypeStruct((256, 16, 128), BF16),
        ),
        in_specs=[hbm] * 9,
        out_specs=(vmem,) * 3,
        scratch_shapes=[
            pltpu.SMEM((ROUNDS,), jnp.int32),
            pltpu.SMEM((ROUNDS, EDGES), jnp.int32),
            pltpu.SMEM((ROUNDS, EDGES), jnp.int32),
            pltpu.SMEM((ROUNDS,), jnp.int32),
            pltpu.VMEM((D, ROWS), F32),
            pltpu.VMEM((1, ROWS), F32),
            pltpu.VMEM((D, NREL), F32),
            pltpu.VMEM((ROUNDS, EDGES), jnp.int32),
            pltpu.VMEM((ROUNDS, EDGES), jnp.int32),
            pltpu.VMEM((ROUNDS, EDGES), jnp.int32),
            pltpu.VMEM((ROUNDS, 1, NEG), jnp.int32),
            pltpu.VMEM((ROWS, WIDE), F32),
            pltpu.VMEM((REL_PAD, WIDE), F32),
            pltpu.VMEM((ROUNDS, EDGES, WIDE), F32),
            pltpu.VMEM((ROUNDS, EDGES, WIDE), F32),
            pltpu.VMEM((ROWS, WIDE), BF16),
            pltpu.VMEM((EDGES, WIDE), BF16),
            pltpu.VMEM((ROWS, WIDE), BF16),
            pltpu.VMEM((EDGES, WIDE), BF16),
            pltpu.VMEM((ROUNDS * EDGES, WIDE), BF16),
            pltpu.VMEM((8 * GROUP, ROUNDS * EDGES), BF16),
            pltpu.VMEM((PACKED, 128), F32),
            tiles(ROUNDS, TILES),
            tiles(CHIPS),
            tiles(CHIPS),
            tiles(ROUNDS, CHIPS),
            tiles(2, ROW_TILES),
            tiles(2, ROW_TILES),
            tiles(2, VEC_TILES),
            tiles(2, VEC_TILES),
            tiles(128),
            tiles(128),
            tiles(128),
            tiles(16, 8),
            tiles(8),
            tiles(8, 8),
            pltpu.SemaphoreType.DMA((ROUNDS, 5)),
            pltpu.SemaphoreType.DMA((ROUNDS, 5)),
            pltpu.SemaphoreType.DMA((4,)),
            pltpu.SemaphoreType.DMA((4,)),
            pltpu.SemaphoreType.DMA((16,)),
            pltpu.SemaphoreType.DMA((16,)),
            pltpu.SemaphoreType.DMA((15,)),
            pltpu.SemaphoreType.DMA((15,)),
            pltpu.SemaphoreType.DMA((12,)),
        ],
        compiler_params=pltpu.CompilerParams(
            collective_id=0, has_side_effects=True, vmem_limit_bytes=60 * 1024 * 1024
        ),
    )(
        round_masks,
        edge_src,
        edge_rel,
        edge_count.reshape(ROUNDS),
        embeddings.T,
        entity_state.reshape(1, ROWS),
        relations.T,
        edge_dst,
        neg_rows,
    )
    new_rows, new_state, new_relations, new_relation_state = pl.pallas_call(
        finish,
        out_shape=(
            jax.ShapeDtypeStruct((D, ROWS), F32),
            jax.ShapeDtypeStruct((ROWS,), F32),
            jax.ShapeDtypeStruct((D, NREL), F32),
            jax.ShapeDtypeStruct((NREL,), F32),
        ),
        in_specs=[hbm] * 5,
        out_specs=(hbm,) * 4,
        scratch_shapes=[
            tiles(256),
            pltpu.VMEM((D, NREL), F32),
            pltpu.VMEM((1, ROWS), F32),
            pltpu.VMEM((NREL,), F32),
            pltpu.VMEM((PACKED, 128), F32),
            pltpu.VMEM((REL_PAD, 128), F32),
            pltpu.VMEM((D, NREL), F32),
            pltpu.VMEM((ROWS,), F32),
            pltpu.VMEM((NREL,), F32),
            pltpu.VMEM((D, ROWS), F32),
            pltpu.SemaphoreType.DMA((9,)),
        ],
        compiler_params=pltpu.CompilerParams(vmem_limit_bytes=60 * 1024 * 1024),
    )(rows_t, state, sums, relations.T, relation_state)
    return (new_rows.T, new_state, new_relations.T, new_relation_state)


def solution(mesh):
    placed = (
        P("dom", None),
        P("dom"),
        P(),
        P(),
        P(),
        P(None, "dom"),
        P(None, "dom"),
        P(None, "dom"),
        P(None, "dom"),
        P(None, "dom", None),
    )
    return jax.shard_map(
        shards,
        mesh=mesh,
        in_specs=placed,
        out_specs=(P("dom", None), P("dom"), P(), P()),
        check_vma=False,
    )
```

```python
import jax
import jax.numpy as jnp
from jax import lax
from jax.experimental import pallas as pl
from jax.experimental.pallas import tpu as pltpu
from jax.sharding import PartitionSpec as P

ROUNDS = 2
D = 400
NREL = 1300
NEG = 1000
ROWS = 256
EDGES = 128
WIDE = 512
LEFT = D - 384
CHIPS = 128
TILES = 76
ROW_TILES = 51
VEC_TILES = 25
REL_PAD = 1408
BLOCK = 1304
GROUP = 168
PACKED = 4096

learning_rate = 0.1

F32 = jnp.float32
BF16 = jnp.bfloat16


def iota(shape, dim):
    return lax.broadcasted_iota(jnp.int32, shape, dim)


def dot(a, b, left=1, right=0):
    return lax.dot_general(a, b, (((left,), (right,)), ((), ())), preferred_element_type=F32)


def halves(value):
    high = value.astype(BF16)
    return high, (value - high.astype(F32)).astype(BF16)


def as_column(row):
    count = row.shape[1]
    square = (count, count)
    return jnp.sum(jnp.where(iota(square, 0) == iota(square, 1), row, 0.0), axis=1, keepdims=True)


def as_row(column):
    count = column.shape[0]
    square = (count, count)
    return jnp.sum(jnp.where(iota(square, 0) == iota(square, 1), column, 0.0), axis=0, keepdims=True)


def remote(source, target, send, recv, device):
    return pltpu.make_async_remote_copy(
        src_ref=source,
        dst_ref=target,
        send_sem=send,
        recv_sem=recv,
        device_id=(device,),
        device_id_type=pl.DeviceIdType.MESH,
    )


def await_bytes(ref, sem):
    pltpu.make_async_copy(ref, ref, sem).wait()


def ring(offset):
    return min(offset, 4 - offset)


OFFSETS = sorted(
    ((dx, dy) for dx in range(4) for dy in range(4)),
    key=lambda offset: -ring(offset[0]) - ring(offset[1]),
)


def row_carrier(tile):
    return (5 * tile) // 2


def vec_carrier(tile):
    return 5 * (tile - ROW_TILES) + 1


def kernel(
    masks_hbm,
    src_hbm,
    rel_hbm,
    counts_hbm,
    emb_hbm,
    state_hbm,
    relations_hbm,
    dst_hbm,
    neg_hbm,
    emb_out,
    state_out,
    gathered,
    masks,
    src_ids,
    rel_ids,
    counts,
    emb_in,
    state_in,
    rel_in,
    src_rows,
    rel_rows,
    dst_rows,
    neg_rows,
    emb,
    relations,
    srcs,
    rels,
    table,
    vec,
    far_table,
    far_vec,
    grads,
    is_rel,
    packed,
    x1,
    held_0,
    held_1,
    x2,
    rows_0,
    rows_1,
    vecs_0,
    vecs_1,
    t0,
    r0,
    t1,
    ra,
    t3,
    rz,
    send,
    recv,
    sum_send,
    sum_recv,
    core_send,
    core_recv,
    gather_send,
    gather_recv,
    loaded,
):
    loads = [
        pltpu.make_async_copy(source, target, loaded.at[n])
        for n, (source, target) in enumerate(
            (
                (emb_hbm, emb_in),
                (relations_hbm, rel_in),
                (src_hbm, src_ids),
                (rel_hbm, rel_ids),
                (masks_hbm, masks),
                (counts_hbm, counts),
                (state_hbm, state_in),
                (src_hbm, src_rows),
                (rel_hbm, rel_rows),
                (dst_hbm, dst_rows),
                (neg_hbm, neg_rows),
            )
        )
    ]
    me = lax.axis_index("dom")
    c = me % 2
    y = (me // 2) % 4
    x = (me // 8) % 4
    z = me // 32
    chip = me // 2
    row_mine = (2 * chip + 1) // 5
    vec_mine = ROW_TILES + chip // 5
    has_row = jnp.logical_and(row_carrier(row_mine) == chip, row_mine < ROW_TILES)
    has_vec = jnp.logical_and(vec_carrier(vec_mine) == chip, vec_mine < TILES)
    active = jnp.logical_or(has_row, has_vec)
    idle = jnp.logical_not(active)

    def plane(step):
        return (z + 4 + ((step + 1) // 2) * (1 - 2 * (step % 2))) % 8

    def over_rows(go):
        def first(at):
            return (32 * at + 4) // 5

        def one_plane(step, _):
            at = plane(step)

            def one(i, _):
                go(i, row_carrier(i))
                return 0

            lax.fori_loop(first(at), jnp.minimum(first(at + 1), ROW_TILES), one, 0)
            return 0

        lax.fori_loop(0, 8, one_plane, 0)

    def over_vecs(go):
        def first(at):
            return (16 * at + 3) // 5

        def one_plane(step, _):
            at = plane(step)

            def one(i, _):
                go(ROW_TILES + i, vec_carrier(ROW_TILES + i))
                return 0

            lax.fori_loop(first(at), jnp.minimum(first(at + 1), VEC_TILES), one, 0)
            return 0

        lax.fori_loop(0, 8, one_plane, 0)

    places = [((x + dx) % 4) * 4 + (y + dy) % 4 for dx, dy in OFFSETS]
    place = places[-1]

    def at_place(to):
        return (z * 16 + to) * 2 + c

    def at_z(to):
        return (to * 16 + place) * 2 + c

    other = me + 1 - 2 * c

    barrier = pltpu.get_barrier_semaphore()

    def tell(device):
        pl.semaphore_signal(barrier, inc=1, device_id=(device,), device_id_type=pl.DeviceIdType.MESH)

    def tell_all(step, _):
        def tell_chip(n, _):
            to = 16 * plane(step) + n

            @pl.when(to != chip)
            def _():
                tell(2 * to + c)

            return 0

        lax.fori_loop(0, 16, tell_chip, 0)
        return 0

    def tell_carrier(i, to):
        tell(2 * to + c)

    @pl.when(active)
    def _():
        lax.fori_loop(0, 8, tell_all, 0)

    @pl.when(idle)
    def _():
        over_rows(tell_carrier)
        over_vecs(tell_carrier)

    for to in places[:-1]:
        tell(at_place(to))
    for step in range(7):
        tell(at_z(plane(step)))
    tell(other)
    for load in loads:
        load.start()

    def gather_rels(r):
        for e in range(EDGES):
            rels[r, e : e + 1, :] = relations[pl.ds(rel_ids[r, e], 1), :]

    def gather_srcs(r):
        for e in range(EDGES):
            srcs[r, e : e + 1, :] = emb[pl.ds(src_ids[r, e], 1), :]

    def hit_row(r):
        hits = jnp.sum((iota((ROWS, NEG), 0) == neg_rows[r]).astype(F32), axis=1, keepdims=True)
        return jnp.concatenate([as_row(hits[:128]), as_row(hits[128:])], axis=1)

    def bucket_rows(r):
        dst = dst_rows[r : r + 1, :].astype(F32)
        live = (iota((1, EDGES), 1) < counts[r]).astype(F32)
        return dst, live, hit_row(r)

    def pack(r, first, rows):
        for i in range(8):
            for j in range(3):
                x1[r, first + 3 * i + j] = rows[16 * i : 16 * i + 16, 128 * j : 128 * j + 128]
        last = rows[:, 384:].astype(F32)
        tail = last[:16]
        for g in range(1, 8):
            tail = tail + pltpu.roll(last[16 * g : 16 * g + 16], LEFT * g, 1)
        x1[r, first + 24] = tail.astype(BF16)

    def unpack(arrived, side, first, target, at):
        for i in range(8):
            for j in range(3):
                target[at + 16 * i : at + 16 * i + 16, 128 * j : 128 * j + 128] = arrived[side, first + 3 * i + j]
        tail = arrived[side, first + 24].astype(F32)
        inside = iota((16, 128), 1) < LEFT
        for g in range(8):
            part = pltpu.roll(tail, 128 - LEFT * g, 1) if g else tail
            target[at + 16 * g : at + 16 * g + 16, 384:] = jnp.where(inside, part, 0.0).astype(BF16)

    def pack_table(r):
        table[...] = emb[...].astype(BF16)
        pack(r, 0, table[0:128, :])
        pack(r, 25, table[128:256, :])

    def pack_vectors(r):
        vec[...] = (srcs[r] * rels[r]).astype(BF16)
        pack(r, ROW_TILES, vec[...])

    def pack_meta(r, rows):
        dst, live, hits = rows
        high = jnp.floor(hits * (1.0 / 16.0))
        low = hits - 16.0 * high
        extras = (dst, live, high[:, :128], high[:, 128:], low[:, :128], low[:, 128:])
        sub = iota((16, 128), 0)
        meta = jnp.zeros((16, 128), F32)
        for n, extra in enumerate(extras):
            meta = jnp.where(sub == n, extra, meta)
        x1[r, 50] = meta.astype(BF16)

    def send_out(r, over):
        held = (held_0, held_1)[r]

        def outward(i, to):
            @pl.when(to != chip)
            def _():
                remote(x1.at[r, i], held.at[chip], send.at[r, 0], recv.at[r, 0], 2 * to + c).start()

            @pl.when(to == chip)
            def _():
                held[chip] = x1[r, i]

        over(outward)

    def relay(r, mask, arrived, mine, sem):
        held = (held_0, held_1)[r]
        chip_mask = lax.shift_right_logical(mask, 1)
        await_bytes(held.at[pl.ds(0, CHIPS - 1)], recv.at[r, 0])

        def onward(step, _):
            base = 16 * plane(step)
            for n in range(16):
                x2[r, base + n] = held[lax.bitwise_xor(chip_mask, base + n)]
            for n in places:
                to = base + n

                @pl.when(to != chip)
                def _():
                    remote(x2.at[r, to], arrived.at[0, mine], send.at[r, 1], recv.at[r, sem], 2 * to + c).start()

            return 0

        lax.fori_loop(0, 8, onward, 0)
        arrived[0, mine] = x2[r, chip]

    def take_in(r, has, arrived, count, sem):
        @pl.when(has)
        def _():
            await_bytes(arrived.at[0, pl.ds(0, count - 1)], recv.at[r, sem])

        @pl.when(jnp.logical_not(has))
        def _():
            await_bytes(arrived.at[0], recv.at[r, sem])

        remote(arrived.at[0], arrived.at[1], send.at[r, sem + 1], recv.at[r, sem + 1], other).start()

    def sent(r):
        @pl.when(active)
        def _():
            await_bytes(x1.at[r, pl.ds(0, TILES - 1)], send.at[r, 0])
            await_bytes(x2.at[r, pl.ds(0, CHIPS - 1)], send.at[r, 1])

        @pl.when(idle)
        def _():
            await_bytes(x1.at[r], send.at[r, 0])

        await_bytes(x1.at[r, pl.ds(0, ROW_TILES)], send.at[r, 2])
        await_bytes(x1.at[r, pl.ds(0, VEC_TILES)], send.at[r, 4])

    def coefficients(vectors, rows, ends):
        dst, live, hits = ends
        scores = dot(vectors, rows, 1, 1)
        dst = as_column(dst)
        live = as_column(live)
        is_dst = iota((EDGES, ROWS), 1).astype(F32) == dst
        neg_coef = (live * (1.0 / (1.0 + jnp.exp(-scores))) / NEG).astype(BF16).astype(F32)
        positive = jnp.sum(jnp.where(is_dst, scores, 0.0), axis=1, keepdims=True)
        pos_coef = -live * (1.0 / (1.0 + jnp.exp(positive)))
        return halves(neg_coef * hits + jnp.where(is_dst, pos_coef, 0.0))

    for load in loads:
        load.wait()
    emb[:, 384:] = jnp.zeros((ROWS, 128), F32)
    for j in range(4):
        depth = min(128, D - 128 * j)
        for i in range(2):
            emb[128 * i : 128 * i + 128, 128 * j : 128 * j + depth] = emb_in[
                128 * j : 128 * j + depth, 128 * i : 128 * i + 128
            ].T
    pack_table(0)
    buckets = [bucket_rows(r) for r in range(ROUNDS)]
    for r in range(ROUNDS):
        pack_meta(r, buckets[r])
    state = jnp.concatenate([as_column(state_in[:, :128]), as_column(state_in[:, 128:])], axis=0)

    gather_srcs(0)
    relations[:, 384:] = jnp.zeros((REL_PAD, 128), F32)
    for j in range(4):
        depth = min(128, D - 128 * j)
        for i in range(11):
            width = min(128, NREL - 128 * i)
            part = rel_in[128 * j : 128 * j + depth, 128 * i : 128 * i + width]
            if width < 128:
                part = jnp.concatenate([part, jnp.ones((depth, 128 - width), F32)], axis=1)
            relations[128 * i : 128 * i + 128, 128 * j : 128 * j + depth] = part.T
    for r in range(ROUNDS):
        gather_rels(r)
    pack_vectors(0)

    @pl.when(active)
    def _():
        pl.semaphore_wait(barrier, CHIPS - 1 + 23)

    @pl.when(idle)
    def _():
        pl.semaphore_wait(barrier, TILES + 23)

    def prepare_sum():
        ids = jnp.concatenate([rel_rows[0:1, :], rel_rows[1:2, :]], axis=1)
        for g in range(8):
            at = GROUP * g
            is_rel[at : at + GROUP, :] = (iota((GROUP, ROUNDS * EDGES), 0) + at == ids).astype(BF16)

    for r in range(ROUNDS):
        mask = masks[r]
        side = lax.bitwise_and(mask, 1)
        far_rows = (rows_0, rows_1)[r]
        far_vecs = (vecs_0, vecs_1)[r]
        send_out(r, over_rows)
        if r > 0:
            gather_srcs(r)
            pack_vectors(r)
        if r + 1 < ROUNDS:
            send_out(r, over_vecs)
            prepare_sum()

        @pl.when(has_row)
        def _():
            relay(r, mask, far_rows, row_mine, 1)

        if r + 1 == ROUNDS:
            send_out(r, over_vecs)
        else:

            @pl.when(has_vec)
            def _():
                relay(r, mask, far_vecs, vec_mine - ROW_TILES, 3)

        take_in(r, has_row, far_rows, ROW_TILES, 1)
        await_bytes(far_rows.at[1], recv.at[r, 2])
        unpack(far_rows, side, 0, far_table, 0)
        unpack(far_rows, side, 25, far_table, 128)
        meta = far_rows[side, 50].astype(F32)
        hits = jnp.concatenate([16.0 * meta[n : n + 1] + meta[n + 2 : n + 3] for n in (2, 3)], axis=1)
        far = (meta[0:1], meta[1:2], hits)

        high, low = coefficients(vec[...], far_table[...], buckets[r])
        if r + 1 < ROUNDS:
            take_in(r, has_vec, far_vecs, VEC_TILES, 3)
        pulled = (dot(high, far_table[...]) + dot(low, far_table[...])).astype(BF16).astype(F32)
        grads[r * EDGES : (r + 1) * EDGES, :] = (pulled * srcs[r]).astype(BF16)

        def update_rows(r, state, pulled, far, far_vecs, side):
            is_src = (iota((ROWS, EDGES), 0) == src_rows[r : r + 1, :]).astype(BF16)
            high, low = halves(pulled * rels[r])
            grad = dot(is_src, high) + dot(is_src, low)
            if r + 1 == ROUNDS:
                take_in(r, has_vec, far_vecs, VEC_TILES, 3)
            await_bytes(far_vecs.at[1], recv.at[r, 4])
            unpack(far_vecs, side, 0, far_vec, 0)
            high, low = coefficients(far_vec[...], table[...], far)
            pushed = dot(high, far_vec[...], 0, 0) + dot(low, far_vec[...], 0, 0)
            grad = grad + pushed.astype(BF16).astype(F32)
            state = state + jnp.sum(grad * grad, axis=1, keepdims=True) * (1.0 / D)
            emb[...] = emb[...] - grad * (learning_rate / jnp.sqrt(state))
            return state

        if r + 1 < ROUNDS:
            state = update_rows(r, state, pulled, far, far_vecs, side)
            pack_table(r + 1)

    tail = jnp.zeros((GROUP, 128), F32)
    for g in range(8):
        rows = min(GROUP, BLOCK - GROUP * g)
        part = dot(is_rel[GROUP * g : GROUP * g + GROUP, :], grads[...])
        for n in range(3):
            at = BLOCK * n + GROUP * g
            packed[at : at + rows, :] = part[:rows, 128 * n : 128 * n + 128]
        end = part[:, 384:]
        tail = tail + (pltpu.roll(end, LEFT * g, 1) if g else end)
    packed[3 * BLOCK : 3 * BLOCK + GROUP, :] = tail
    packed[3 * BLOCK + GROUP :, :] = jnp.zeros((PACKED - 3 * BLOCK - GROUP, 128), F32)

    def partial(half, to):
        rows = pl.ds(pl.multiple_of(2048 * half + 128 * to, 128), 128)
        return packed[rows, :].reshape(8, 16, 128)

    for k, to in enumerate(places):
        piece = pl.ds(8 * to, 8)
        t0[piece] = partial(1 - c, to).astype(BF16)
        remote(t0.at[piece], r0.at[piece], core_send.at[k], core_recv.at[k], other).start()
    for k, to in enumerate(places):
        piece = pl.ds(8 * to, 8)
        await_bytes(r0.at[piece], core_recv.at[k])
        t1[piece] = (partial(c, to) + r0[piece].astype(F32)).astype(BF16)
        if k < 15:
            remote(t1.at[piece], ra.at[place], sum_send.at[0], sum_recv.at[0], at_place(to)).start()
    ra[place] = t1[pl.ds(8 * place, 8)]

    @pl.when(has_vec)
    def _():
        relay(r, mask, far_vecs, vec_mine - ROW_TILES, 3)

    await_bytes(ra.at[pl.ds(0, 15)], sum_recv.at[0])

    def added(ref, count):
        total = ref[0].astype(F32)
        for n in range(1, count):
            total = total + ref[n].astype(F32)
        return total.astype(BF16)

    t3[...] = added(ra, 16)
    for step in range(7):
        remote(t3, rz.at[z], sum_send.at[1], sum_recv.at[1], at_z(plane(step))).start()
    rz[z] = t3[...]
    await_bytes(rz.at[pl.ds(0, 7)], sum_recv.at[1])

    base = c * 128 + 8 * place
    gathered[pl.ds(base, 8)] = added(rz, 8)
    own = gathered.at[pl.ds(base, 8)]
    for k, to in enumerate(places[:-1]):
        dx, dy = OFFSETS[k]
        back = OFFSETS.index((-dx % 4, -dy % 4))
        remote(own, own, gather_send.at[k], gather_recv.at[back], at_place(to)).start()
    remote(own, own, sum_send.at[3], sum_recv.at[3], other).start()
    state = update_rows(r, state, pulled, far, far_vecs, side)
    for k, to in enumerate(places[:-1]):
        piece = gathered.at[pl.ds(c * 128 + 8 * to, 8)]
        await_bytes(piece, gather_recv.at[k])
        remote(piece, piece, sum_send.at[3], sum_recv.at[3], other).start()
    for j in range(4):
        depth = min(128, D - 128 * j)
        for i in range(2):
            part = emb[128 * i : 128 * i + 128, 128 * j : 128 * j + 128].T
            emb_out[128 * j : 128 * j + depth, 128 * i : 128 * i + 128] = part[:depth]
    state_out[...] = jnp.concatenate([as_row(state[:128]), as_row(state[128:])], axis=1)
    await_bytes(gathered.at[pl.ds(0, 128)], sum_recv.at[3])

    for r in range(ROUNDS):
        sent(r)
    for k in range(16):
        await_bytes(r0.at[pl.ds(0, 8)], core_send.at[k])
    for n, tiles in ((0, 120), (1, 56), (3, 128)):
        await_bytes(gathered.at[pl.ds(0, tiles)], sum_send.at[n])
    for k in range(15):
        await_bytes(gathered.at[pl.ds(0, 8)], gather_send.at[k])


def finish(
    emb_hbm,
    state_hbm,
    sums_hbm,
    rel_hbm,
    rel_state_hbm,
    emb_out,
    state_out,
    rel_out,
    rel_state_out,
    sums,
    rel_in,
    state_in,
    rel_state_in,
    packed,
    tails,
    rel_new,
    state_new,
    rel_state_new,
    emb_kept,
    sems,
):
    loads = [
        pltpu.make_async_copy(sums_hbm, sums, sems.at[0]),
        pltpu.make_async_copy(rel_state_hbm, rel_state_in, sems.at[1]),
        pltpu.make_async_copy(rel_hbm, rel_in, sems.at[2]),
        pltpu.make_async_copy(state_hbm, state_in, sems.at[3]),
    ]
    loads.append(pltpu.make_async_copy(emb_hbm, emb_kept, sems.at[4]))
    for load in loads:
        load.start()
    for load in loads[:2]:
        load.wait()
    packed[...] = sums[...].astype(F32).reshape(PACKED, 128)
    for load in loads[2:]:
        load.wait()
    state_new[...] = state_in[...].reshape(ROWS)
    stores = [
        pltpu.make_async_copy(state_new, state_out, sems.at[5]),
        pltpu.make_async_copy(emb_kept, emb_out, sems.at[8]),
    ]
    for store in stores:
        store.start()
    end = packed[3 * BLOCK : 3 * BLOCK + GROUP, :]
    inside = iota((GROUP, 128), 1) < LEFT
    for g in range(8):
        part = pltpu.roll(end, 128 - LEFT * g, 1) if g else end
        tails[GROUP * g : GROUP * g + GROUP, :] = jnp.where(inside, part, 0.0)
    tails[8 * GROUP :, :] = jnp.zeros((REL_PAD - 8 * GROUP, 128), F32)
    for i in range(11):
        at = 128 * i
        width = min(128, NREL - at)
        rows = min(128, BLOCK - at)
        parts = [packed[BLOCK * n + at : BLOCK * n + at + rows, :] for n in range(3)] + [tails[at : at + rows, :]]
        if rows < 128:
            parts = [jnp.concatenate([part, jnp.zeros((128 - rows, 128), F32)], axis=0) for part in parts]
        old = rel_state_in[at : at + width].reshape(1, width)
        if width < 128:
            old = jnp.concatenate([old, jnp.ones((1, 128 - width), F32)], axis=1)
        squares = parts[0] * parts[0] + parts[1] * parts[1] + parts[2] * parts[2] + parts[3] * parts[3]
        fresh = old + as_row(jnp.sum(squares, axis=1, keepdims=True)) * (1.0 / D)
        rel_state_new[at : at + width] = fresh[:, :width].reshape(width)
        scale = learning_rate / jnp.sqrt(fresh)
        for n in range(4):
            depth = min(128, D - 128 * n)
            change = parts[n].T[:depth] * scale
            cols = slice(128 * n, 128 * n + depth)
            rel_new[cols, at : at + width] = rel_in[cols, at : at + width] - change[:, :width]
        if i in (3, 7, 10):
            done = pl.ds(512 * (i // 4), min(512, NREL - 512 * (i // 4)))
            part = pltpu.make_async_copy(rel_new.at[:, done], rel_out.at[:, done], sems.at[9 + i // 4])
            part.start()
            stores.append(part)
    stores.append(pltpu.make_async_copy(rel_state_new, rel_state_out, sems.at[7]))
    stores[-1].start()
    for store in stores:
        store.wait()


def shards(
    embeddings,
    entity_state,
    relations,
    relation_state,
    round_masks,
    edge_src,
    edge_rel,
    edge_dst,
    edge_count,
    neg_rows,
):
    vmem = pl.BlockSpec(memory_space=pltpu.VMEM)

    def tiles(*lead):
        return pltpu.VMEM(lead + (16, 128), BF16)

    hbm = pl.BlockSpec(memory_space=pltpu.HBM)
    rows_t, state, sums = pl.pallas_call(
        kernel,
        out_shape=(
            jax.ShapeDtypeStruct((D, ROWS), F32),
            jax.ShapeDtypeStruct((1, ROWS), F32),
            jax.ShapeDtypeStruct((256, 16, 128), BF16),
        ),
        in_specs=[hbm] * 9,
        out_specs=(vmem,) * 3,
        scratch_shapes=[
            pltpu.SMEM((ROUNDS,), jnp.int32),
            pltpu.SMEM((ROUNDS, EDGES), jnp.int32),
            pltpu.SMEM((ROUNDS, EDGES), jnp.int32),
            pltpu.SMEM((ROUNDS,), jnp.int32),
            pltpu.VMEM((D, ROWS), F32),
            pltpu.VMEM((1, ROWS), F32),
            pltpu.VMEM((D, NREL), F32),
            pltpu.VMEM((ROUNDS, EDGES), jnp.int32),
            pltpu.VMEM((ROUNDS, EDGES), jnp.int32),
            pltpu.VMEM((ROUNDS, EDGES), jnp.int32),
            pltpu.VMEM((ROUNDS, 1, NEG), jnp.int32),
            pltpu.VMEM((ROWS, WIDE), F32),
            pltpu.VMEM((REL_PAD, WIDE), F32),
            pltpu.VMEM((ROUNDS, EDGES, WIDE), F32),
            pltpu.VMEM((ROUNDS, EDGES, WIDE), F32),
            pltpu.VMEM((ROWS, WIDE), BF16),
            pltpu.VMEM((EDGES, WIDE), BF16),
            pltpu.VMEM((ROWS, WIDE), BF16),
            pltpu.VMEM((EDGES, WIDE), BF16),
            pltpu.VMEM((ROUNDS * EDGES, WIDE), BF16),
            pltpu.VMEM((8 * GROUP, ROUNDS * EDGES), BF16),
            pltpu.VMEM((PACKED, 128), F32),
            tiles(ROUNDS, TILES),
            tiles(CHIPS),
            tiles(CHIPS),
            tiles(ROUNDS, CHIPS),
            tiles(2, ROW_TILES),
            tiles(2, ROW_TILES),
            tiles(2, VEC_TILES),
            tiles(2, VEC_TILES),
            tiles(128),
            tiles(128),
            tiles(128),
            tiles(16, 8),
            tiles(8),
            tiles(8, 8),
            pltpu.SemaphoreType.DMA((ROUNDS, 5)),
            pltpu.SemaphoreType.DMA((ROUNDS, 5)),
            pltpu.SemaphoreType.DMA((4,)),
            pltpu.SemaphoreType.DMA((4,)),
            pltpu.SemaphoreType.DMA((16,)),
            pltpu.SemaphoreType.DMA((16,)),
            pltpu.SemaphoreType.DMA((15,)),
            pltpu.SemaphoreType.DMA((15,)),
            pltpu.SemaphoreType.DMA((12,)),
        ],
        compiler_params=pltpu.CompilerParams(
            collective_id=0, has_side_effects=True, vmem_limit_bytes=60 * 1024 * 1024
        ),
    )(
        round_masks,
        edge_src,
        edge_rel,
        edge_count.reshape(ROUNDS),
        embeddings.T,
        entity_state.reshape(1, ROWS),
        relations.T,
        edge_dst,
        neg_rows,
    )
    new_rows, new_state, new_relations, new_relation_state = pl.pallas_call(
        finish,
        out_shape=(
            jax.ShapeDtypeStruct((D, ROWS), F32),
            jax.ShapeDtypeStruct((ROWS,), F32),
            jax.ShapeDtypeStruct((D, NREL), F32),
            jax.ShapeDtypeStruct((NREL,), F32),
        ),
        in_specs=[hbm] * 5,
        out_specs=(hbm,) * 4,
        scratch_shapes=[
            tiles(256),
            pltpu.VMEM((D, NREL), F32),
            pltpu.VMEM((1, ROWS), F32),
            pltpu.VMEM((NREL,), F32),
            pltpu.VMEM((PACKED, 128), F32),
            pltpu.VMEM((REL_PAD, 128), F32),
            pltpu.VMEM((D, NREL), F32),
            pltpu.VMEM((ROWS,), F32),
            pltpu.VMEM((NREL,), F32),
            pltpu.VMEM((D, ROWS), F32),
            pltpu.SemaphoreType.DMA((12,)),
        ],
        compiler_params=pltpu.CompilerParams(vmem_limit_bytes=60 * 1024 * 1024),
    )(rows_t, state, sums, relations.T, relation_state)
    return (new_rows.T, new_state, new_relations.T, new_relation_state)


def solution(mesh):
    placed = (
        P("dom", None),
        P("dom"),
        P(),
        P(),
        P(),
        P(None, "dom"),
        P(None, "dom"),
        P(None, "dom"),
        P(None, "dom"),
        P(None, "dom", None),
    )
    return jax.shard_map(
        shards,
        mesh=mesh,
        in_specs=placed,
        out_specs=(P("dom", None), P("dom"), P(), P()),
        check_vma=False,
    )
```
